128 devices in a mesh: occ: 4 (over x), virt: 32 (over y, z, core).
Axes of the slice: x: 4, y: 4, z: 4, core: 2. Of those that a mesh axis runs over, the one named last changes fastest.
Arguments:
- amplitudes: bfloat16 [1, 100, 1024, 1024], P(None, 'occ', 'virt'), may hold values from -6 to 6
- cycle_block: bfloat16 [1024, 100, 4, 1024], P('virt', None, 'occ'), may hold values from -0.01953125 to 0.01953125
- drive_term: bfloat16 [1, 1024, 4, 1024], P(None, 'virt', 'occ'), may hold values from -6 to 6
- occ_energy: float32 [100], replicated, may hold values from -2 to -0.3
- virt_energy: float32 [1024], replicated, may hold values from 0.2 to 4
- occ_irrep: int32 [100], replicated, may hold values from 0 to 1
- virt_irrep: int32 [1024], replicated, may hold values from 0 to 1
- slab_occ: int32 [1], replicated, may hold values from 0 to 99
- col_occ: int32 [4], replicated, may hold values from 0 to 99
Outputs:
- amp_update: float32 [1, 1024, 4, 1024], P(None, 'virt', 'occ')
The draws below stay inside these ranges and needn't reach their ends.
Inputs may be any that keep to these rules, and one draw needn't show every extreme that they name: `occ_irrep`: labels of the two irreducible representations of the C2 group. `virt_irrep`: labels of the two irreducible representations of the C2 group.
All inputs are finite; a program needn't handle non-finite values.
Results may differ from the reference program's by a relative error of at most 0.0003.
Values may be sent and summed in bfloat16 or wider, within the bound.
A program may use at most 64 MiB of HBM per device.

```python
import jax
import jax.numpy as jnp

O = 100
V = 1024
SI = 1
JO = 4


def touch_ends(array, rng, least, high):
    longest = array.shape.index(max(array.shape))
    spots = []
    for shift in (0, 1):
        where = [jax.random.randint(jax.random.fold_in(rng, axis), (), 0, length) for axis, length in enumerate(array.shape)]
        where[longest] = (where[longest] + shift) % array.shape[longest]
        spots.append(tuple(where))
    return array.at[spots[0]].set(least).at[spots[1]].set(high)


def block_levels(key, shape, shards, low, high):
    def one(axis_at, parts):
        draws = jax.random.uniform(jax.random.fold_in(jax.random.fold_in(key, 6), axis_at), (parts,), jnp.float32, low / len(shards), high / len(shards))
        return jnp.repeat(jnp.exp(draws), shape[axis_at] // parts).reshape((-1,) + (1,) * (len(shape) - axis_at - 1))

    gain = one(*shards[0])
    for cut in shards[1:]:
        gain = gain * one(*cut)
    return gain


def gaussian(key, dims, scale, reach, pieces=(), held_as=jnp.bfloat16):
    values = jax.random.normal(key, dims, jnp.float32) * scale
    if len(pieces) > 0:
        values = block_levels(key, dims, pieces, -0.22, 0.18) * values
    return jnp.clip(values, min=-reach, max=reach).astype(held_as)


def setup_inputs(seed: int = 0) -> dict:
    seeds = jax.random.split(jax.random.key(seed), 10)
    return {
        "amplitudes": gaussian(seeds[0], (SI, O, V, V), 1.0, 6.0, ((1, 4), (2, 32))),
        "cycle_block": gaussian(seeds[1], (V, O, JO, V), (O * V) ** -0.5, 0.01953125, ((0, 32), (2, 4))),
        "drive_term": gaussian(seeds[2], (SI, V, JO, V), 1.0, 6.0, ((1, 32), (2, 4))),
        "occ_energy": jnp.clip(jax.random.uniform(seeds[3], (O,), jnp.float32, -2.0, -0.3), -2.0, -0.3),
        "virt_energy": jnp.clip(jax.random.uniform(seeds[4], (V,), jnp.float32, 0.2, 4.0), 0.2, 4.0),
        "occ_irrep": touch_ends(jax.random.randint(seeds[5], (O,), 0, 2), jax.random.fold_in(seeds[5], 1), 0, 1).astype(jnp.int32),
        "virt_irrep": touch_ends(jax.random.randint(seeds[6], (V,), 0, 2), jax.random.fold_in(seeds[6], 1), 0, 1).astype(jnp.int32),
        "slab_occ": jax.random.randint(seeds[7], (SI,), 0, O).astype(jnp.int32),
        "col_occ": touch_ends(jax.random.randint(seeds[8], (JO,), 0, O), jax.random.fold_in(seeds[8], 1), 0, O - 1).astype(jnp.int32),
    }


def reference(amplitudes, cycle_block, drive_term, occ_energy, virt_energy, occ_irrep, virt_irrep, slab_occ, col_occ):
    slab_irrep = occ_irrep[slab_occ]
    col_irrep = occ_irrep[col_occ]
    parity = slab_irrep[:, None, None, None] + occ_irrep[None, :, None, None] + virt_irrep[None, None, :, None] + virt_irrep[None, None, None, :]
    masked = jnp.where(parity % 2 == 0, amplitudes, jnp.zeros_like(amplitudes))
    left = jnp.transpose(masked, (0, 2, 3, 1)).reshape(SI * V, V * O)
    right = cycle_block.reshape(V * O, JO * V)
    cycle_sum = jnp.dot(left, right, preferred_element_type=jnp.float32).reshape(SI, V, JO, V)
    divisor = (virt_energy[None, :, None, None] + virt_energy[None, None, None, :]
               - occ_energy[slab_occ][:, None, None, None] - occ_energy[col_occ][None, None, :, None])
    out_parity = slab_irrep[:, None, None, None] + virt_irrep[None, :, None, None] + col_irrep[None, None, :, None] + virt_irrep[None, None, None, :]
    value = (drive_term.astype(jnp.float32) + cycle_sum) / divisor
    return jnp.where(out_parity % 2 == 0, value, jnp.zeros_like(value))
```

```python
import functools

import jax
import jax.numpy as jnp
from jax import lax
from jax.experimental import pallas as pl
from jax.experimental.pallas import tpu as pltpu
from jax.sharding import PartitionSpec as P

MESH = pl.DeviceIdType.MESH
CAP = 304
CAPL = 320
MCAP = 640
NSTEP = 6
BF = jnp.bfloat16
F32 = jnp.float32


def pick_entries(values_table, indices):
    hits = indices[:, None] == jnp.arange(values_table.shape[0], dtype=jnp.int32)[None, :]
    return jnp.sum(
        jnp.where(hits, values_table[None, :], jnp.zeros((), values_table.dtype)), axis=1
    )


def general_cycle(amplitudes, cycle_block, occ_irrep, virt_irrep, slab_irrep):
    k_rows = amplitudes.shape[1]
    a_cols = amplitudes.shape[2]
    occ_pos = lax.axis_index("occ")
    virt_pos = lax.axis_index("virt")
    irr_k = lax.dynamic_slice_in_dim(occ_irrep, occ_pos * k_rows, k_rows)
    irr_a = lax.dynamic_slice_in_dim(virt_irrep, virt_pos * a_cols, a_cols)
    parity = (
        slab_irrep[:, None, None, None]
        + irr_k[None, :, None, None]
        + irr_a[None, None, :, None]
        + virt_irrep[None, None, None, :]
    )
    masked = jnp.where(parity % 2 == 0, amplitudes, jnp.zeros((), amplitudes.dtype))
    pair_block = lax.all_gather(masked, "occ", axis=1, tiled=True)
    relaid = lax.all_to_all(pair_block, "virt", split_axis=3, concat_axis=2, tiled=True)
    partial_value = jnp.einsum(
        "skac,ckjb->sajb", relaid, cycle_block, preferred_element_type=jnp.float32
    )
    cycle_sum = lax.psum_scatter(partial_value, "virt", scatter_dimension=1, tiled=True)
    return cycle_sum[0, :, 0, :]


def block_transpose(tiles, b1, b0):
    t = list(tiles)
    for q in (0, 1):
        a, b = t[q], t[q + 2]
        t[q] = jnp.where(b1, pltpu.roll(b, 64, 1), a)
        t[q + 2] = jnp.where(b1, b, pltpu.roll(a, 64, 1))
    for q in (0, 2):
        a, b = t[q], t[q + 1]
        t[q] = jnp.where(b0, pltpu.roll(b, 32, 1), a)
        t[q + 1] = jnp.where(b0, b, pltpu.roll(a, 96, 1))
    return t


def kernel(
    occ_ref, amp, wraw, rank_ref, cls_ref, rankb_ref, amask, wmask, lclass,
    out,
    wv, wf, wrep, fold, unfold, foldb, unfoldb, clsb, mbuf, sbuf, sleft, abuf, aleft,
    xbuf, xleft, zacc, crecv, tsum, t2, r1buf, r2buf, fin,
    wsem, ysend, yrecv, yloc, ysendl, yrecvl, ylocl,
    zsend, zrecv, zloc, zsendl, zrecvl, zlocl,
    xsend, xrecv, fsend, frecv, xsendl, xrecvl, fsendl, frecvl,
    csend, crecvs, r1send, r1recv, r2send, r2recv,
):
    x = lax.axis_index("occ")
    v = lax.axis_index("virt")
    y = v // 8
    z = (v // 2) % 4
    core = v % 2
    me8 = z * 2 + core

    def virt_at(yy, zz, cc):
        return (yy * 4 + zz) * 2 + cc

    right = (x + 1) % 4
    left = (x + 3) % 4

    def y_peer(o):
        return (x, virt_at((y + o) % 4, z, core))

    def z_peer(o):
        oz, oc = o // 2, o % 2
        return (x, virt_at(y, (z + oz) % 4, (core + oc) % 2))

    def z_slot(o):
        return ((z + o // 2) % 4) * 2 + (core + o % 2) % 2

    def remote(src, dst, ssem, rsem, dev):
        return pltpu.make_async_remote_copy(
            src_ref=src, dst_ref=dst, send_sem=ssem, recv_sem=rsem,
            device_id=dev, device_id_type=MESH,
        )

    def y_src(h, k0, nk, yd):
        return amp.at[pl.ds(k0, nk), pl.ds(16 * h, 16), pl.ds(pl.multiple_of(256 * yd, 256), 256)]

    def y_dst(h, k0, nk):
        return mbuf.at[h, pl.ds(k0, nk), pl.ds(pl.multiple_of(16 * y, 16), 16), :]

    def y_copy(n, o):
        h, g = n // 3, n % 3
        return remote(y_src(h, 8 * g, 8, (y + o) % 4), y_dst(h, 8 * g, 8),
                      ysend.at[n, o - 1], yrecv.at[n, o - 1], y_peer(o))

    def y_copyl(h, o):
        return remote(y_src(h, 24, 1, (y + o) % 4), y_dst(h, 24, 1),
                      ysendl.at[h, o - 1], yrecvl.at[h, o - 1], y_peer(o))

    def y_own(n):
        h, g = n // 3, n % 3
        return pltpu.make_async_copy(y_src(h, 8 * g, 8, y), y_dst(h, 8 * g, 8), yloc.at[n])

    def y_ownl(h):
        return pltpu.make_async_copy(y_src(h, 24, 1, y), y_dst(h, 24, 1), ylocl.at[h])

    def z_dst(n):
        return abuf.at[n, pl.ds(pl.multiple_of(64 * me8, 64), 64), :]

    def z_dstl(h):
        return aleft.at[h, pl.ds(pl.multiple_of(16 * me8, 16), 16), :]

    def z_copy(n, o):
        return remote(sbuf.at[n, z_slot(o)], z_dst(n), zsend.at[n, o - 1], zrecv.at[n, o - 1], z_peer(o))

    def z_copyl(h, o):
        return remote(sleft.at[h, z_slot(o)], z_dstl(h), zsendl.at[h, o - 1], zrecvl.at[h, o - 1], z_peer(o))

    def z_own(n):
        return pltpu.make_async_copy(sbuf.at[n, me8], z_dst(n), zloc.at[n])

    def z_ownl(h):
        return pltpu.make_async_copy(sleft.at[h, me8], z_dstl(h), zlocl.at[h])

    def x_copy(n, side):
        return remote(xbuf.at[n, 0], xbuf.at[n, 1 + side], xsend.at[n, side], xrecv.at[n, side],
                      ((right, left)[side], v))

    def f_copy(n, side):
        lanes = pl.ds(128 * side, 128)
        return remote(xbuf.at[n, 1 + side, :, lanes], xbuf.at[n, 3, :, lanes],
                      fsend.at[n, side], frecv.at[n, side], ((right, left)[side], v))

    def x_copyl(h, side):
        return remote(xleft.at[h, 0], xleft.at[h, 1 + side], xsendl.at[h, side], xrecvl.at[h, side],
                      ((right, left)[side], v))

    def f_copyl(h, side):
        return remote(xleft.at[h, 1 + side], xleft.at[h, 3], fsendl.at[h], frecvl.at[h],
                      ((right, left)[side], v))

    def c_copy(h):
        return remote(zacc.at[h, :, 1 - core], crecv.at[h], csend.at[h], crecvs.at[h],
                      (x, virt_at(y, z, 1 - core)))

    def r1_copy(h, axis, o):
        if axis == 0:
            yd = (y + o) % 4
            return remote(tsum.at[h, 0, :, yd], r1buf.at[h, 0, o - 1], r1send.at[h, o - 1],
                          r1recv.at[h, o - 1], (x, virt_at(yd, z, core)))
        zd = (z + o) % 4
        return remote(tsum.at[h, 1, zd], r1buf.at[h, 1, o - 1], r1send.at[h, 2 + o],
                      r1recv.at[h, 2 + o], (x, virt_at(y, zd, core)))

    def r2_copy(h, axis, o):
        if axis == 0:
            zd = (z + o) % 4
            return remote(t2.at[h, 0, zd], r2buf.at[h, 0, o - 1], r2send.at[h, o - 1],
                          r2recv.at[h, o - 1], (x, virt_at(y, zd, core)))
        yd = (y + o) % 4
        return remote(t2.at[h, 1, yd], r2buf.at[h, 1, o - 1], r2send.at[h, 2 + o],
                      r2recv.at[h, 2 + o], (x, virt_at(yd, z, core)))

    barrier = pltpu.get_barrier_semaphore()
    peers = [y_peer(o) for o in (1, 2, 3)] + [z_peer(o) for o in range(1, 8)] + [(right, v), (left, v)]
    for dev in peers:
        pl.semaphore_signal(barrier, inc=1, device_id=dev, device_id_type=MESH)
    pl.semaphore_wait(barrier, len(peers))

    def w_copy(i):
        rows = pl.ds(800 * i, 800)
        return pltpu.make_async_copy(wraw.at[rows], wv.at[rows], wsem.at[i])

    for n in range(NSTEP):
        for o in (2, 1, 3):
            y_copy(n, o).start()
        y_own(n).start()
        if n % 3 == 2:
            for o in (2, 1, 3):
                y_copyl(n // 3, o).start()
            y_ownl(n // 3).start()
        if n == 1:
            for i in range(4):
                w_copy(i).start()

    for h in range(2):
        row = rank_ref[h]
        fold[h] = (lax.broadcasted_iota(jnp.int32, (CAPL, 512), 0).astype(F32) == row).astype(F32).astype(BF)
        col = jnp.transpose(jnp.broadcast_to(row, (128, 512)))
        for t in range(3):
            w = min(128, CAPL - 128 * t)
            lane = lax.broadcasted_iota(jnp.int32, (512, w), 1).astype(F32) + 128.0 * t
            unfold[h, :, 128 * t:128 * t + w] = (col[:, :w] == lane).astype(F32).astype(BF)
        clsb[h] = jnp.transpose(jnp.broadcast_to(cls_ref[h], (128, 512)))
    rowb = rankb_ref[...]
    unfoldb[...] = (lax.broadcasted_iota(jnp.int32, (MCAP, 1024), 0).astype(F32) == rowb).astype(F32).astype(BF)
    colb = jnp.transpose(jnp.broadcast_to(rowb, (128, 1024)))
    for t in range(MCAP // 128):
        lane = lax.broadcasted_iota(jnp.int32, (1024, 128), 1).astype(F32) + 128.0 * t
        foldb[:, 128 * t:128 * t + 128] = (colb == lane).astype(F32).astype(BF)

    lane128 = lax.broadcasted_iota(jnp.int32, (1, 128), 1)

    def prepare_w(j, carry):
        for q in range(4):
            par = occ_ref[4 * j + q]
            rows = pl.ds(pl.multiple_of(128 * j + 32 * q, 32), 32)
            wv[rows, :] = wv[rows, :] * wmask[par]
        rows = pl.ds(pl.multiple_of(128 * j, 128), 128)
        wf[rows, :] = jnp.dot(wv[rows, :], foldb[...], preferred_element_type=F32).astype(BF)
        return carry

    def relay(n):
        h, g = n // 3, n % 3
        for o in (1, 2, 3):
            y_copy(n, o).wait_recv()
        y_own(n).wait()
        b1 = (lane128 // 64) % 2 == 1
        b0 = (lane128 // 32) % 2 == 1
        for kg in range(2):
            rowsq = []
            for q in range(4):
                k = 8 * g + 4 * kg + q
                par = occ_ref[25 * x + k]
                rowsq.append((mbuf[h, k] * amask[h, par]).astype(F32))
            for t in range(2):
                res = block_transpose([r[:, 128 * t:128 * t + 128] for r in rowsq], b1, b0)
                for d in range(4):
                    sbuf[n, 4 * t + d, :, 128 * kg:128 * kg + 128] = res[d].astype(BF)
        for o in (4, 5, 2, 3, 6, 7, 1):
            z_copy(n, o).start()
        z_own(n).start()

        @pl.when(g == 2)
        def _():
            for o in (1, 2, 3):
                y_copyl(h, o).wait_recv()
            y_ownl(h).wait()
            par = occ_ref[25 * x + 24]
            whole = (mbuf[h, 24] * amask[h, par]).astype(F32)
            for t in range(2):
                res = block_transpose(
                    [whole[16 * q:16 * q + 16, 128 * t:128 * t + 128] for q in range(4)], b1, b0)
                for d in range(4):
                    sleft[h, 4 * t + d] = res[d].astype(BF)
            for o in (4, 5, 2, 3, 6, 7, 1):
                z_copyl(h, o).start()
            z_ownl(h).start()

    def fold_step(n):
        h, g = n // 3, n % 3
        for o in range(1, 8):
            z_copy(n, o).wait_recv()
        z_own(n).wait()
        xbuf[n, 0] = jnp.dot(fold[h, :CAP], abuf[n], preferred_element_type=F32).astype(BF)
        for side in range(2):
            x_copy(n, side).start()

        @pl.when(g == 2)
        def _():
            for o in range(1, 8):
                z_copyl(h, o).wait_recv()
            z_ownl(h).wait()
            got = aleft[h].astype(F32)
            parts = []
            for s in range(8):
                for q in range(4):
                    parts.append(jnp.where(lane128 // 32 == q, got[16 * s:16 * s + 16], 0.0))
            spread = jnp.concatenate(parts, axis=0).astype(BF)
            both = jnp.dot(fold[h], spread, preferred_element_type=F32)
            both = both + pltpu.roll(both, 64, 1)
            both = both + pltpu.roll(both, 32, 1)
            packed = both[0:80]
            for q in range(1, 4):
                packed = jnp.where(lane128 // 32 == q, both[80 * q:80 * q + 80], packed)
            xleft[h, 0] = packed.astype(BF)
            for side in range(2):
                x_copyl(h, side).start()

    def product(n, slot, first):
        h, g = n // 3, n % 3
        src = (x + (0, 3, 1, 2)[slot]) % 4
        part = jnp.dot(unfold[h, :, :CAP], xbuf[n, slot], preferred_element_type=F32)
        cls = clsb[h]
        lane_cls = lclass[4 * src + g]
        part = jnp.concatenate(
            [jnp.where(cls == lane_cls[:, 128 * t:128 * t + 128], part[:, 128 * t:128 * t + 128], 0.0)
             for t in range(2)], axis=1).astype(BF)
        rows = pl.ds(pl.multiple_of(800 * src + 256 * g, 32), 256)
        value = jnp.dot(part, wf[rows, :], preferred_element_type=F32)
        for zz in range(4):
            for cc in range(2):
                r0 = (zz * 2 + cc) * 64
                if first:
                    zacc[h, zz, cc] = value[r0:r0 + 64]
                else:
                    zacc[h, zz, cc] += value[r0:r0 + 64]

    def product_left(h, slot):
        src = (x + (0, 3, 1, 2)[slot]) % 4
        got = xleft[h, slot].astype(F32)
        spread = jnp.concatenate(
            [jnp.where(lane128 // 32 == q, got, 0.0) for q in range(4)], axis=0).astype(BF)
        part = jnp.dot(unfold[h], spread, preferred_element_type=F32)
        lane_cls = lclass[4 * src + 3]
        part = jnp.where(clsb[h] == lane_cls[:, :128], part, 0.0).astype(BF)
        one = wf[pl.ds(pl.multiple_of(800 * src + 768, 32), 32), :]
        value = jnp.dot(part, jnp.concatenate([one] * 4, axis=0), preferred_element_type=F32)
        for zz in range(4):
            for cc in range(2):
                r0 = (zz * 2 + cc) * 64
                zacc[h, zz, cc] += value[r0:r0 + 64]

    def near_step(n):
        h, g = n // 3, n % 3
        for side in range(2):
            x_copy(n, side).wait_recv()
            f_copy(n, side).start()

        @pl.when(g == 2)
        def _():
            for side in range(2):
                x_copyl(h, side).wait_recv()

            @pl.when(h == 0)
            def _():
                f_copyl(h, 0).start()

            @pl.when(h == 1)
            def _():
                f_copyl(h, 1).start()

        @pl.when(g == 0)
        def _():
            zacc[h] = jnp.zeros_like(zacc[h])

        for slot in range(3):
            product(n, slot, False)

        @pl.when(g == 2)
        def _():
            for slot in range(3):
                product_left(h, slot)

    def far_step(n):
        h, g = n // 3, n % 3
        for side in range(2):
            f_copy(n, side).wait_recv()
        product(n, 3, False)

        @pl.when(g == 2)
        def _():
            f_copyl(h, 0).wait_recv()
            product_left(h, 3)
            c_copy(h).start()

    def sum_core(h):
        c_copy(h).wait_recv()
        for zz in range(4):
            both = zacc[h, zz, core] + crecv[h, zz]
            for yy in range(4):
                for rh in range(2):
                    r0 = yy * 16 + rh * 8
                    tsum[h, rh, zz, yy] = both[r0:r0 + 8]
        for axis in range(2):
            for o in (2, 1, 3):
                r1_copy(h, axis, o).start()

    def sum_first(h):
        for axis in range(2):
            for o in (1, 2, 3):
                r1_copy(h, axis, o).wait_recv()
        for i in range(4):
            t2[h, 0, i] = tsum[h, 0, i, y] + r1buf[h, 0, 0, i] + r1buf[h, 0, 1, i] + r1buf[h, 0, 2, i]
            t2[h, 1, i] = tsum[h, 1, z, i] + r1buf[h, 1, 0, i] + r1buf[h, 1, 1, i] + r1buf[h, 1, 2, i]
        for axis in range(2):
            for o in (2, 1, 3):
                r2_copy(h, axis, o).start()

    def sum_second(h):
        for axis in range(2):
            for o in (1, 2, 3):
                r2_copy(h, axis, o).wait_recv()
        fin[h, 0] = t2[h, 0, z] + r2buf[h, 0, 0] + r2buf[h, 0, 1] + r2buf[h, 0, 2]
        fin[h, 1] = t2[h, 1, y] + r2buf[h, 1, 0] + r2buf[h, 1, 1] + r2buf[h, 1, 2]

    def step(n, carry):
        @pl.when(n < NSTEP)
        def _():
            relay(n)

        @pl.when(n == 0)
        def _():
            for i in range(4):
                w_copy(i).wait()
            lax.fori_loop(0, 13, prepare_w, 0)

        @pl.when(jnp.logical_and(n >= 1, n < NSTEP + 1))
        def _():
            fold_step(n - 1)

        @pl.when(n == 1)
        def _():
            lax.fori_loop(13, 25, prepare_w, 0)

        @pl.when(jnp.logical_and(n >= 2, n < NSTEP + 2))
        def _():
            near_step(n - 2)

        @pl.when(jnp.logical_or(n == 6, n == 9))
        def _():
            sum_core(n // 3 - 2)

        @pl.when(jnp.logical_or(n == 7, n == 10))
        def _():
            sum_first(n // 3 - 2)

        @pl.when(jnp.logical_and(n >= 3, n < NSTEP + 3))
        def _():
            far_step(n - 3)

        return carry

    lax.fori_loop(0, 11, step, 0)
    sum_second(0)
    sum_second(1)

    total = jnp.concatenate([fin[0, 0], fin[0, 1], fin[1, 0], fin[1, 1]], axis=0)
    hi = total.astype(BF)
    rest = total - hi.astype(F32)
    mid = rest.astype(BF)
    low = (rest - mid.astype(F32)).astype(BF)
    table = unfoldb[...]
    out[...] = (
        jnp.dot(hi, table, preferred_element_type=F32)
        + jnp.dot(mid, table, preferred_element_type=F32)
    ) + jnp.dot(low, table, preferred_element_type=F32)

    def finish(n, carry):
        for o in (1, 2, 3):
            y_copy(n, o).wait_send()
        for o in range(1, 8):
            z_copy(n, o).wait_send()
        for side in range(2):
            x_copy(n, side).wait_send()
            f_copy(n, side).wait_send()
        return carry

    lax.fori_loop(0, NSTEP, finish, 0)

    def finish_half(h, carry):
        for o in (1, 2, 3):
            y_copyl(h, o).wait_send()
        for o in range(1, 8):
            z_copyl(h, o).wait_send()
        for side in range(2):
            x_copyl(h, side).wait_send()
        f_copyl(h, 0).wait_send()
        c_copy(h).wait_send()
        for axis in range(2):
            for o in (1, 2, 3):
                r1_copy(h, axis, o).wait_send()
                r2_copy(h, axis, o).wait_send()
        return carry

    lax.fori_loop(0, 2, finish_half, 0)


def folded_cycle(amplitudes, cycle_block, occ_irrep, virt_irrep, slab_irrep, col_irrep_here, rank_half, rank_all):
    x = lax.axis_index("occ")
    v = lax.axis_index("virt")
    y, z, core = v // 8, (v // 2) % 4, v % 2
    slab = slab_irrep[0]
    amp = amplitudes.reshape(25, 32, 1024)
    wraw = jnp.transpose(cycle_block, (1, 2, 0, 3)).reshape(3200, 1024)
    vi = virt_irrep.reshape(4, 4, 2, 2, 16)
    half_cls = jnp.transpose(vi, (3, 1, 2, 0, 4)).reshape(2, 1, 512).astype(F32)
    mine = lax.dynamic_slice(vi, (0, z, core, 0, 0), (4, 1, 1, 2, 16)).reshape(4, 2, 16)
    row_par = jnp.transpose(mine, (1, 0, 2)).reshape(2, 64)
    c_mid = lax.dynamic_slice_in_dim(virt_irrep, 256 * y, 256)
    two = jnp.arange(2, dtype=jnp.int32)
    amask = (
        (slab + two[None, :, None, None] + row_par[:, None, :, None] + c_mid[None, None, None, :]) % 2 == 0
    ).astype(BF)
    c_here = lax.dynamic_slice_in_dim(virt_irrep, 32 * v, 32)
    wmask = (
        (two[:, None, None] + c_here[None, :, None] + virt_irrep[None, None, :] + col_irrep_here) % 2 == 0
    ).astype(BF)
    kk = occ_irrep.reshape(4, 25)
    main = (kk[:, :24, None] + c_here[None, None, :] + slab).reshape(4, 3, 256)
    last = jnp.broadcast_to(kk[:, 24:, None, None] + c_here[None, None, None, :] + slab, (4, 1, 8, 32)).reshape(4, 1, 256)
    lclass = (jnp.concatenate([main, last], axis=1) % 2).reshape(16, 1, 256).astype(F32)

    dma = pltpu.SemaphoreType.DMA
    vmem = pl.BlockSpec(memory_space=pltpu.VMEM)
    hbm = pl.BlockSpec(memory_space=pl.ANY)
    scratch = [
        pltpu.VMEM((3200, 1024), BF),
        pltpu.VMEM((3200, MCAP), BF),
        pltpu.VMEM((8, 128), BF),
        pltpu.VMEM((2, CAPL, 512), BF),
        pltpu.VMEM((2, 512, CAPL), BF),
        pltpu.VMEM((1024, MCAP), BF),
        pltpu.VMEM((MCAP, 1024), BF),
        pltpu.VMEM((2, 512, 128), F32),
        pltpu.VMEM((2, 25, 64, 256), BF),
        pltpu.VMEM((NSTEP, 8, 64, 256), BF),
        pltpu.VMEM((2, 8, 16, 128), BF),
        pltpu.VMEM((NSTEP, 512, 256), BF),
        pltpu.VMEM((2, 128, 128), BF),
        pltpu.VMEM((NSTEP, 4, CAP, 256), BF),
        pltpu.VMEM((2, 4, 80, 128), BF),
        pltpu.VMEM((2, 4, 2, 64, MCAP), F32),
        pltpu.VMEM((2, 4, 64, MCAP), F32),
        pltpu.VMEM((2, 2, 4, 4, 8, MCAP), F32),
        pltpu.VMEM((2, 2, 4, 8, MCAP), F32),
        pltpu.VMEM((2, 2, 3, 4, 8, MCAP), F32),
        pltpu.VMEM((2, 2, 3, 8, MCAP), F32),
        pltpu.VMEM((2, 2, 8, MCAP), F32),
        dma((4,)),
        dma((NSTEP, 3)), dma((NSTEP, 3)), dma((NSTEP,)),
        dma((2, 3)), dma((2, 3)), dma((2,)),
        dma((NSTEP, 7)), dma((NSTEP, 7)), dma((NSTEP,)),
        dma((2, 7)), dma((2, 7)), dma((2,)),
        dma((NSTEP, 2)), dma((NSTEP, 2)), dma((NSTEP, 2)), dma((NSTEP, 2)),
        dma((2, 2)), dma((2, 2)), dma((2,)), dma((2,)),
        dma((2,)), dma((2,)),
        dma((2, 6)), dma((2, 6)), dma((2, 6)), dma((2, 6)),
    ]
    return pl.pallas_call(
        kernel,
        out_shape=jax.ShapeDtypeStruct((32, 1024), F32),
        in_specs=[pl.BlockSpec(memory_space=pltpu.SMEM), hbm, hbm] + [vmem] * 6,
        out_specs=vmem,
        scratch_shapes=scratch,
        compiler_params=pltpu.CompilerParams(
            collective_id=0, has_side_effects=True, vmem_limit_bytes=52 * 2**20
        ),
        name="cycle",
    )(occ_irrep, amp, wraw, rank_half, half_cls, rank_all, amask, wmask, lclass)


def ranks(cls):
    n = cls.shape[-1]
    same = cls[..., :, None] == cls[..., None, :]
    before = jnp.arange(n)[:, None] < jnp.arange(n)[None, :]
    return jnp.sum(jnp.where(same & before, 1, 0), axis=-2, dtype=jnp.int32)


def body(
    amplitudes,
    cycle_block,
    drive_term,
    occ_energy,
    virt_energy,
    occ_irrep,
    virt_irrep,
    slab_occ,
    col_occ,
):
    a_cols = amplitudes.shape[2]
    j_cols = cycle_block.shape[2]
    occ_pos = lax.axis_index("occ")
    virt_pos = lax.axis_index("virt")
    slab_irrep = pick_entries(occ_irrep, slab_occ)
    col_irrep = pick_entries(occ_irrep, col_occ)
    irr_a = lax.dynamic_slice_in_dim(virt_irrep, virt_pos * a_cols, a_cols)
    irr_cols = lax.dynamic_slice_in_dim(col_irrep, occ_pos * j_cols, j_cols)

    half = jnp.transpose(virt_irrep.reshape(4, 4, 2, 2, 16), (3, 1, 2, 0, 4)).reshape(2, 512)
    rank_half = ranks(half)
    rank_all = ranks(virt_irrep)
    fits = jnp.logical_and(jnp.max(rank_half) < CAP, jnp.max(rank_all) < MCAP)

    cycle_sum = lax.cond(
        fits,
        lambda *args: folded_cycle(*args),
        lambda amp, w, occ, virt, slab, *rest: general_cycle(amp, w, occ, virt, slab),
        amplitudes, cycle_block, occ_irrep, virt_irrep, slab_irrep, irr_cols[0],
        rank_half.reshape(2, 1, 512).astype(F32), rank_all.reshape(1, 1024).astype(F32),
    )
    cycle_sum = cycle_sum.reshape(1, a_cols, j_cols, 1024)

    e_slab = pick_entries(occ_energy, slab_occ)
    e_cols = lax.dynamic_slice_in_dim(pick_entries(occ_energy, col_occ), occ_pos * j_cols, j_cols)
    e_rows = lax.dynamic_slice_in_dim(virt_energy, virt_pos * a_cols, a_cols)
    divisor = (
        e_rows[None, :, None, None]
        + virt_energy[None, None, None, :]
        - e_slab[:, None, None, None]
        - e_cols[None, None, :, None]
    )
    out_parity = (
        slab_irrep[:, None, None, None]
        + irr_a[None, :, None, None]
        + irr_cols[None, None, :, None]
        + virt_irrep[None, None, None, :]
    )
    value = (drive_term.astype(jnp.float32) + cycle_sum) / divisor
    return jnp.where(out_parity % 2 == 0, value, jnp.zeros((), jnp.float32))


def solution(mesh):
    in_specs = (
        P(None, "occ", "virt", None),
        P("virt", None, "occ", None),
        P(None, "virt", "occ", None),
        P(),
        P(),
        P(),
        P(),
        P(),
        P(),
    )
    out_specs = P(None, "virt", "occ", None)
    return jax.shard_map(body, mesh=mesh, in_specs=in_specs, out_specs=out_specs, check_vma=False)
```

```python
import jax
import jax.numpy as jnp
from jax import lax
from jax.experimental import pallas as pl
from jax.experimental.pallas import tpu as pltpu
from jax.sharding import PartitionSpec as P

MESH = pl.DeviceIdType.MESH
CAP = 304
CAPL = 320
MCAP = 640
NSTEP = 6
OUT = (1, 32, 1, 1024)
BF = jnp.bfloat16
F32 = jnp.float32


def pick_entries(values_table, indices):
    hits = indices[:, None] == jnp.arange(values_table.shape[0], dtype=jnp.int32)[None, :]
    return jnp.sum(
        jnp.where(hits, values_table[None, :], jnp.zeros((), values_table.dtype)), axis=1
    )


def spread_all(block, axis, count):
    return lax.all_to_all(jnp.broadcast_to(block[None], (count,) + block.shape), axis, 0, 0, tiled=True)


def general_update(amp, wraw, drive, occ_irrep, virt_irrep, slab_occ, col_occ, occ_energy, virt_energy):
    x = lax.axis_index("occ")
    v = lax.axis_index("virt")
    slab_irrep = pick_entries(occ_irrep, slab_occ)[0]
    col_here = lax.dynamic_slice_in_dim(col_occ, x, 1)
    col_irrep = pick_entries(occ_irrep, col_here)[0]
    irr_k = lax.dynamic_slice_in_dim(occ_irrep, x * 25, 25)
    irr_a = lax.dynamic_slice_in_dim(virt_irrep, v * 32, 32)
    parity = slab_irrep + irr_k[:, None, None] + irr_a[None, :, None] + virt_irrep[None, None, :]
    masked = jnp.where(parity % 2 == 0, amp, jnp.zeros((), amp.dtype))
    pair_block = spread_all(masked, "occ", 4).reshape(100, 32, 1024)
    relaid = lax.all_to_all(pair_block, "virt", split_axis=2, concat_axis=1, tiled=True)
    w = wraw.reshape(100, 32, 1024)
    partial_value = jnp.einsum("kac,kcb->ab", relaid, w, preferred_element_type=F32)
    parts = lax.all_to_all(partial_value.reshape(32, 32, 1024), "virt", 0, 0, tiled=True)
    cycle_sum = jnp.sum(parts, axis=0)
    e_slab = pick_entries(occ_energy, slab_occ)[0]
    e_col = pick_entries(occ_energy, col_here)[0]
    e_rows = lax.dynamic_slice_in_dim(virt_energy, v * 32, 32)
    divisor = e_rows[:, None] + virt_energy[None, :] - e_slab - e_col
    out_parity = slab_irrep + irr_a[:, None] + col_irrep + virt_irrep[None, :]
    value = (drive.astype(F32) + cycle_sum) / divisor
    return jnp.where(out_parity % 2 == 0, value, jnp.zeros((), F32)).reshape(OUT)


def block_transpose(tiles, b1, b0):
    t = list(tiles)
    for q in (0, 1):
        a, b = t[q], t[q + 2]
        t[q] = jnp.where(b1, pltpu.roll(b, 64, 1), a)
        t[q + 2] = jnp.where(b1, b, pltpu.roll(a, 64, 1))
    for q in (0, 2):
        a, b = t[q], t[q + 1]
        t[q] = jnp.where(b0, pltpu.roll(b, 32, 1), a)
        t[q + 1] = jnp.where(b0, b, pltpu.roll(a, 96, 1))
    return t


def kernel(
    occ_ref, slab_ref, colo_ref, eocc_ref, virt_ref, evirt_ref, drive_ref, amp, wraw,
    out,
    wv, wf, amask, wmask, vrow, col, crow, rankb, rankh, fold, unfold, foldb, unfoldb, clsb, mbuf, sbuf, sleft, abuf, aleft,
    xbuf, xleft, zacc, crecv, tsum, t2, r1buf, r2buf, fin, ecol,
    wsem, ysend, yrecv, yloc, ysendl, yrecvl, ylocl,
    zsend, zrecv, zloc, zsendl, zrecvl, zlocl,
    xsend, xrecv, fsend, frecv, xsendl, xrecvl, fsendl, frecvl,
    csend, crecvs, r1send, r1recv, r2send, r2recv,
):
    x = lax.axis_index("occ")
    v = lax.axis_index("virt")
    y = v // 8
    z = (v // 2) % 4
    core = v % 2
    me8 = z * 2 + core

    def virt_at(yy, zz, cc):
        return (yy * 4 + zz) * 2 + cc

    right = (x + 1) % 4
    left = (x + 3) % 4

    def y_peer(o):
        return (x, virt_at((y + o) % 4, z, core))

    def z_peer(o):
        oz, oc = o // 2, o % 2
        return (x, virt_at(y, (z + oz) % 4, (core + oc) % 2))

    def z_slot(o):
        return ((z + o // 2) % 4) * 2 + (core + o % 2) % 2

    def remote(src, dst, ssem, rsem, dev):
        return pltpu.make_async_remote_copy(
            src_ref=src, dst_ref=dst, send_sem=ssem, recv_sem=rsem,
            device_id=dev, device_id_type=MESH,
        )

    def y_src(h, k0, nk, yd):
        return amp.at[pl.ds(k0, nk), pl.ds(16 * h, 16), pl.ds(pl.multiple_of(256 * yd, 256), 256)]

    def y_dst(h, k0, nk):
        return mbuf.at[h, pl.ds(k0, nk), pl.ds(pl.multiple_of(16 * y, 16), 16), :]

    def y_copy(n, o):
        h, g = n // 3, n % 3
        return remote(y_src(h, 8 * g, 8, (y + o) % 4), y_dst(h, 8 * g, 8),
                      ysend.at[n, o - 1], yrecv.at[n, o - 1], y_peer(o))

    def y_copyl(h, o):
        return remote(y_src(h, 24, 1, (y + o) % 4), y_dst(h, 24, 1),
                      ysendl.at[h, o - 1], yrecvl.at[h, o - 1], y_peer(o))

    def y_own(n):
        h, g = n // 3, n % 3
        return pltpu.make_async_copy(y_src(h, 8 * g, 8, y), y_dst(h, 8 * g, 8), yloc.at[n])

    def y_ownl(h):
        return pltpu.make_async_copy(y_src(h, 24, 1, y), y_dst(h, 24, 1), ylocl.at[h])

    def z_dst(n):
        return abuf.at[n, pl.ds(pl.multiple_of(64 * me8, 64), 64), :]

    def z_dstl(h):
        return aleft.at[h, pl.ds(pl.multiple_of(16 * me8, 16), 16), :]

    def z_copy(n, o):
        return remote(sbuf.at[n, z_slot(o)], z_dst(n), zsend.at[n, o - 1], zrecv.at[n, o - 1], z_peer(o))

    def z_copyl(h, o):
        return remote(sleft.at[h, z_slot(o)], z_dstl(h), zsendl.at[h, o - 1], zrecvl.at[h, o - 1], z_peer(o))

    def z_own(n):
        return pltpu.make_async_copy(sbuf.at[n, me8], z_dst(n), zloc.at[n])

    def z_ownl(h):
        return pltpu.make_async_copy(sleft.at[h, me8], z_dstl(h), zlocl.at[h])

    def x_copy(n, side):
        return remote(xbuf.at[n, 0], xbuf.at[n, 1 + side], xsend.at[n, side], xrecv.at[n, side],
                      ((right, left)[side], v))

    def f_copy(n, side):
        lanes = pl.ds(128 * side, 128)
        return remote(xbuf.at[n, 1 + side, :, lanes], xbuf.at[n, 3, :, lanes],
                      fsend.at[n, side], frecv.at[n, side], ((right, left)[side], v))

    def x_copyl(h, side):
        return remote(xleft.at[h, 0], xleft.at[h, 1 + side], xsendl.at[h, side], xrecvl.at[h, side],
                      ((right, left)[side], v))

    def f_copyl(h, side):
        return remote(xleft.at[h, 1 + side], xleft.at[h, 3], fsendl.at[h], frecvl.at[h],
                      ((right, left)[side], v))

    def c_copy(h):
        return remote(zacc.at[h, :, 1 - core], crecv.at[h], csend.at[h], crecvs.at[h],
                      (x, virt_at(y, z, 1 - core)))

    def r1_copy(h, axis, o):
        if axis == 0:
            yd = (y + o) % 4
            return remote(tsum.at[h, 0, :, yd], r1buf.at[h, 0, o - 1], r1send.at[h, o - 1],
                          r1recv.at[h, o - 1], (x, virt_at(yd, z, core)))
        zd = (z + o) % 4
        return remote(tsum.at[h, 1, zd], r1buf.at[h, 1, o - 1], r1send.at[h, 2 + o],
                      r1recv.at[h, 2 + o], (x, virt_at(y, zd, core)))

    def r2_copy(h, axis, o):
        if axis == 0:
            zd = (z + o) % 4
            return remote(t2.at[h, 0, zd], r2buf.at[h, 0, o - 1], r2send.at[h, o - 1],
                          r2recv.at[h, o - 1], (x, virt_at(y, zd, core)))
        yd = (y + o) % 4
        return remote(t2.at[h, 1, yd], r2buf.at[h, 1, o - 1], r2send.at[h, 2 + o],
                      r2recv.at[h, 2 + o], (x, virt_at(yd, z, core)))

    barrier = pltpu.get_barrier_semaphore()
    peers = [y_peer(o) for o in (1, 2, 3)] + [z_peer(o) for o in range(1, 8)] + [(right, v), (left, v)]
    for dev in peers:
        pl.semaphore_signal(barrier, inc=1, device_id=dev, device_id_type=MESH)
    pl.semaphore_wait(barrier, len(peers))

    def w_copy(i):
        rows = pl.ds(800 * i, 800)
        return pltpu.make_async_copy(wraw.at[rows], wv.at[rows], wsem.at[i])

    for n in range(NSTEP):
        for o in (2, 1, 3):
            y_copy(n, o).start()
        y_own(n).start()
        if n % 3 == 2:
            for o in (2, 1, 3):
                y_copyl(n // 3, o).start()
            y_ownl(n // 3).start()
        if n == 1:
            for i in range(4):
                w_copy(i).start()

    lane128 = lax.broadcasted_iota(jnp.int32, (1, 128), 1)

    slab = slab_ref[0]
    slab_irr = occ_ref[slab]
    colo = colo_ref[x]
    col_irr = occ_ref[colo]

    def flip(row, par):
        return jnp.where(par % 2 == 1, 1.0 - row, row)

    def one_hot(cond):
        return cond.astype(F32).astype(BF)

    vrow[...] = virt_ref[...].astype(F32)
    col[...] = jnp.transpose(jnp.broadcast_to(vrow[...], (128, 1024)))
    for h in range(2):
        rows = jnp.concatenate(
            [col[pl.ds(pl.multiple_of(256 * yy + 32 * (me8) + 16 * h, 16), 16), :] for yy in range(4)], axis=0)
        for t in range(2):
            c_mid = vrow[:, pl.ds(pl.multiple_of(256 * y + 128 * t, 128), 128)]
            for par in range(2):
                amask[h, par, :, 128 * t:128 * t + 128] = one_hot(rows == flip(c_mid, slab_irr + par))

    def rank_tables():
        def chunk(i, carry):
            rows = lax.broadcasted_iota(jnp.int32, (128, 1024), 0) + 128 * i
            cols = lax.broadcasted_iota(jnp.int32, (128, 1024), 1)
            before = cols < rows
            ones = col[...].astype(BF)
            count = jnp.dot(one_hot(before), ones, preferred_element_type=F32)
            same = ((rows ^ cols) & 16) == 0
            count_h = jnp.dot(one_hot(before & same), ones, preferred_element_type=F32)
            here = pl.ds(pl.multiple_of(128 * i, 128), 128)
            cls = col[here, :]
            rows = lax.broadcasted_iota(jnp.int32, (128, 128), 0) + 128 * i
            rankb[here, :] = jnp.where(cls == 1.0, count, rows.astype(F32) - count)
            rows_h = (rows >> 5) * 16 + (rows & 15)
            count_h = jnp.where(cls == 1.0, count_h, rows_h.astype(F32) - count_h)
            for b in range(8):
                place = (((i % 2) * 4 + b // 2) * 4 + i // 2) * 16
                rankh[b % 2, pl.ds(pl.multiple_of(place, 16), 16), :] = count_h[16 * b:16 * b + 16]
                clsb[b % 2, pl.ds(pl.multiple_of(place, 16), 16), :] = cls[16 * b:16 * b + 16]
            return carry

        lax.fori_loop(0, 8, chunk, 0)
        for h in range(2):
            row = jnp.transpose(rankh[h])[0:1]
            fold[h] = one_hot(lax.broadcasted_iota(jnp.int32, (CAPL, 512), 0).astype(F32) == row)

    def more_tables():
        for h in range(2):
            for t in range(3):
                w = min(128, CAPL - 128 * t)
                lane = lax.broadcasted_iota(jnp.int32, (512, w), 1).astype(F32) + 128.0 * t
                unfold[h, :, 128 * t:128 * t + w] = one_hot(rankh[h][:, :w] == lane)
        for t in range(MCAP // 128):
            lane = lax.broadcasted_iota(jnp.int32, (1024, 128), 1).astype(F32) + 128.0 * t
            foldb[:, 128 * t:128 * t + 128] = one_hot(rankb[...] == lane)
        crows = col[pl.ds(pl.multiple_of(32 * v, 32), 32), :]
        for par in range(2):
            for t in range(8):
                row = flip(vrow[:, 128 * t:128 * t + 128], col_irr + par)
                wmask[par, :, 128 * t:128 * t + 128] = one_hot(crows == row)
        sub = lax.broadcasted_iota(jnp.int32, (32, 128), 0)
        hit = sub == lax.broadcasted_iota(jnp.int32, (32, 128), 1) % 32
        crow[...] = jnp.sum(jnp.where(hit, crows, 0.0), axis=0, keepdims=True)

    def last_tables():
        row = jnp.transpose(rankb[...])[0:1]
        unfoldb[...] = one_hot(lax.broadcasted_iota(jnp.int32, (MCAP, 1024), 0).astype(F32) == row)

    def lane_class(src, k0, step):
        row = flip(crow[...], slab_irr + occ_ref[25 * src + k0])
        for q in range(1, 4):
            other = flip(crow[...], slab_irr + occ_ref[25 * src + k0 + q * step])
            row = jnp.where(lane128 // 32 == q, other, row)
        return row

    def prepare_w(j, carry):
        for q in range(4):
            par = occ_ref[4 * j + q]
            rows = pl.ds(pl.multiple_of(128 * j + 32 * q, 32), 32)
            wv[rows, :] = wv[rows, :] * wmask[par]
        rows = pl.ds(pl.multiple_of(128 * j, 128), 128)
        wf[rows, :] = jnp.dot(wv[rows, :], foldb[...], preferred_element_type=F32).astype(BF)
        return carry

    def relay(n):
        h, g = n // 3, n % 3
        for o in (1, 2, 3):
            y_copy(n, o).wait_recv()
        y_own(n).wait()
        b1 = (lane128 // 64) % 2 == 1
        b0 = (lane128 // 32) % 2 == 1
        for kg in range(2):
            rowsq = []
            for q in range(4):
                k = 8 * g + 4 * kg + q
                par = occ_ref[25 * x + k]
                rowsq.append((mbuf[h, k] * amask[h, par]).astype(F32))
            for t in range(2):
                res = block_transpose([r[:, 128 * t:128 * t + 128] for r in rowsq], b1, b0)
                for d in range(4):
                    sbuf[n, 4 * t + d, :, 128 * kg:128 * kg + 128] = res[d].astype(BF)
        for o in (4, 5, 2, 3, 6, 7, 1):
            z_copy(n, o).start()
        z_own(n).start()

        @pl.when(g == 2)
        def _():
            for o in (1, 2, 3):
                y_copyl(h, o).wait_recv()
            y_ownl(h).wait()
            par = occ_ref[25 * x + 24]
            whole = (mbuf[h, 24] * amask[h, par]).astype(F32)
            for t in range(2):
                res = block_transpose(
                    [whole[16 * q:16 * q + 16, 128 * t:128 * t + 128] for q in range(4)], b1, b0)
                for d in range(4):
                    sleft[h, 4 * t + d] = res[d].astype(BF)
            for o in (4, 5, 2, 3, 6, 7, 1):
                z_copyl(h, o).start()
            z_ownl(h).start()

    def fold_step(n):
        h, g = n // 3, n % 3
        for o in range(1, 8):
            z_copy(n, o).wait_recv()
        z_own(n).wait()
        xbuf[n, 0] = jnp.dot(fold[h, :CAP], abuf[n], preferred_element_type=F32).astype(BF)
        for side in range(2):
            x_copy(n, side).start()

        @pl.when(g == 2)
        def _():
            for o in range(1, 8):
                z_copyl(h, o).wait_recv()
            z_ownl(h).wait()
            got = aleft[h].astype(F32)
            parts = []
            for s in range(8):
                for q in range(4):
                    parts.append(jnp.where(lane128 // 32 == q, got[16 * s:16 * s + 16], 0.0))
            spread = jnp.concatenate(parts, axis=0).astype(BF)
            both = jnp.dot(fold[h], spread, preferred_element_type=F32)
            both = both + pltpu.roll(both, 64, 1)
            both = both + pltpu.roll(both, 32, 1)
            packed = both[0:80]
            for q in range(1, 4):
                packed = jnp.where(lane128 // 32 == q, both[80 * q:80 * q + 80], packed)
            xleft[h, 0] = packed.astype(BF)
            for side in range(2):
                x_copyl(h, side).start()

    def product(n, slot):
        h, g = n // 3, n % 3
        src = (x + (0, 3, 1, 2)[slot]) % 4
        part = jnp.dot(unfold[h, :, :CAP], xbuf[n, slot], preferred_element_type=F32)
        cls = clsb[h]
        part = jnp.concatenate(
            [jnp.where(cls == lane_class(src, 8 * g + 4 * t, 1), part[:, 128 * t:128 * t + 128], 0.0)
             for t in range(2)], axis=1).astype(BF)
        rows = pl.ds(pl.multiple_of(800 * src + 256 * g, 32), 256)
        value = jnp.dot(part, wf[rows, :], preferred_element_type=F32)
        for zz in range(4):
            for cc in range(2):
                r0 = (zz * 2 + cc) * 64
                zacc[h, zz, cc] += value[r0:r0 + 64]

    def product_left(h, slot):
        src = (x + (0, 3, 1, 2)[slot]) % 4
        got = xleft[h, slot].astype(F32)
        spread = jnp.concatenate(
            [jnp.where(lane128 // 32 == q, got, 0.0) for q in range(4)], axis=0).astype(BF)
        part = jnp.dot(unfold[h], spread, preferred_element_type=F32)
        part = jnp.where(clsb[h] == lane_class(src, 24, 0), part, 0.0).astype(BF)
        one = wf[pl.ds(pl.multiple_of(800 * src + 768, 32), 32), :]
        value = jnp.dot(part, jnp.concatenate([one] * 4, axis=0), preferred_element_type=F32)
        for zz in range(4):
            for cc in range(2):
                r0 = (zz * 2 + cc) * 64
                zacc[h, zz, cc] += value[r0:r0 + 64]

    def near_step(n):
        h, g = n // 3, n % 3
        for side in range(2):
            x_copy(n, side).wait_recv()
            f_copy(n, side).start()

        @pl.when(g == 2)
        def _():
            for side in range(2):
                x_copyl(h, side).wait_recv()

            @pl.when(h == 0)
            def _():
                f_copyl(h, 0).start()

            @pl.when(h == 1)
            def _():
                f_copyl(h, 1).start()

        @pl.when(g == 0)
        def _():
            zacc[h] = jnp.zeros_like(zacc[h])

        for slot in range(3):
            product(n, slot)

        @pl.when(g == 2)
        def _():
            for slot in range(3):
                product_left(h, slot)

    def far_step(n):
        h, g = n // 3, n % 3
        for side in range(2):
            f_copy(n, side).wait_recv()
        product(n, 3)

        @pl.when(g == 2)
        def _():
            f_copyl(h, 0).wait_recv()
            product_left(h, 3)
            c_copy(h).start()

    def sum_core(h):
        c_copy(h).wait_recv()
        for zz in range(4):
            both = zacc[h, zz, core] + crecv[h, zz]
            for yy in range(4):
                for rh in range(2):
                    r0 = yy * 16 + rh * 8
                    tsum[h, rh, zz, yy] = both[r0:r0 + 8]
        for axis in range(2):
            for o in (2, 1, 3):
                r1_copy(h, axis, o).start()

    def sum_first(h):
        for axis in range(2):
            for o in (1, 2, 3):
                r1_copy(h, axis, o).wait_recv()
        for i in range(4):
            t2[h, 0, i] = tsum[h, 0, i, y] + r1buf[h, 0, 0, i] + r1buf[h, 0, 1, i] + r1buf[h, 0, 2, i]
            t2[h, 1, i] = tsum[h, 1, z, i] + r1buf[h, 1, 0, i] + r1buf[h, 1, 1, i] + r1buf[h, 1, 2, i]
        for axis in range(2):
            for o in (2, 1, 3):
                r2_copy(h, axis, o).start()

    def sum_second(h):
        for axis in range(2):
            for o in (1, 2, 3):
                r2_copy(h, axis, o).wait_recv()
        fin[h, 0] = t2[h, 0, z] + r2buf[h, 0, 0] + r2buf[h, 0, 1] + r2buf[h, 0, 2]
        fin[h, 1] = t2[h, 1, y] + r2buf[h, 1, 0] + r2buf[h, 1, 1] + r2buf[h, 1, 2]

    def step(n, carry):
        @pl.when(n < NSTEP)
        def _():
            relay(n)

        @pl.when(n == 0)
        def _():
            rank_tables()

        @pl.when(jnp.logical_and(n >= 1, n < NSTEP + 1))
        def _():
            fold_step(n - 1)

        @pl.when(n == 1)
        def _():
            more_tables()
            for i in range(4):
                w_copy(i).wait()
            lax.fori_loop(0, 9, prepare_w, 0)

        @pl.when(n == 2)
        def _():
            lax.fori_loop(9, 25, prepare_w, 0)

        @pl.when(n == 3)
        def _():
            last_tables()

        @pl.when(jnp.logical_and(n >= 2, n < NSTEP + 2))
        def _():
            near_step(n - 2)

        @pl.when(jnp.logical_or(n == 6, n == 9))
        def _():
            sum_core(n // 3 - 2)

        @pl.when(jnp.logical_or(n == 7, n == 10))
        def _():
            sum_first(n // 3 - 2)

        @pl.when(jnp.logical_and(n >= 3, n < NSTEP + 3))
        def _():
            far_step(n - 3)

        return carry

    lax.fori_loop(0, 11, step, 0)
    sum_second(0)
    sum_second(1)

    total = jnp.concatenate([fin[0, 0], fin[0, 1], fin[1, 0], fin[1, 1]], axis=0)
    hi = total.astype(BF)
    rest = total - hi.astype(F32)
    mid = rest.astype(BF)
    low = (rest - mid.astype(F32)).astype(BF)
    tile = evirt_ref[:, pl.ds(pl.multiple_of(128 * (v // 4), 128), 128)]
    e_rows = jnp.transpose(jnp.broadcast_to(tile, (128, 128)))
    ecol[...] = e_rows
    e_here = ecol[pl.ds(pl.multiple_of(32 * (v % 4), 32), 32), :]
    e_slab = eocc_ref[slab]
    e_col = eocc_ref[colo]
    cls = col[pl.ds(pl.multiple_of(32 * v, 32), 32), :]
    for t in range(8):
        lanes = slice(128 * t, 128 * t + 128)
        table = unfoldb[:, lanes]
        cycle_sum = (
            jnp.dot(hi, table, preferred_element_type=F32)
            + jnp.dot(mid, table, preferred_element_type=F32)
        ) + jnp.dot(low, table, preferred_element_type=F32)
        divisor = e_here + evirt_ref[:, lanes] - e_slab - e_col
        value = (drive_ref[:, lanes].astype(F32) + cycle_sum) / divisor
        out[0, :, 0, lanes] = jnp.where(cls == flip(vrow[:, lanes], slab_irr + col_irr), value, 0.0)

    def finish(n, carry):
        for o in (1, 2, 3):
            y_copy(n, o).wait_send()
        for o in range(1, 8):
            z_copy(n, o).wait_send()
        for side in range(2):
            x_copy(n, side).wait_send()
            f_copy(n, side).wait_send()
        return carry

    lax.fori_loop(0, NSTEP, finish, 0)

    def finish_half(h, carry):
        for o in (1, 2, 3):
            y_copyl(h, o).wait_send()
        for o in range(1, 8):
            z_copyl(h, o).wait_send()
        for side in range(2):
            x_copyl(h, side).wait_send()
        f_copyl(h, 0).wait_send()
        c_copy(h).wait_send()
        for axis in range(2):
            for o in (1, 2, 3):
                r1_copy(h, axis, o).wait_send()
                r2_copy(h, axis, o).wait_send()
        return carry

    lax.fori_loop(0, 2, finish_half, 0)


def folded_update(amp, wraw, drive, occ_irrep, virt_irrep, slab_occ, col_occ, occ_energy, virt_energy):
    dma = pltpu.SemaphoreType.DMA
    vmem = pl.BlockSpec(memory_space=pltpu.VMEM)
    hbm = pl.BlockSpec(memory_space=pl.ANY)
    scratch = [
        pltpu.VMEM((3200, 1024), BF),
        pltpu.VMEM((3200, MCAP), BF),
        pltpu.VMEM((2, 2, 64, 256), BF),
        pltpu.VMEM((2, 32, 1024), BF),
        pltpu.VMEM((1, 1024), F32),
        pltpu.VMEM((1024, 128), F32),
        pltpu.VMEM((1, 128), F32),
        pltpu.VMEM((1024, 128), F32),
        pltpu.VMEM((2, 512, 128), F32),
        pltpu.VMEM((2, CAPL, 512), BF),
        pltpu.VMEM((2, 512, CAPL), BF),
        pltpu.VMEM((1024, MCAP), BF),
        pltpu.VMEM((MCAP, 1024), BF),
        pltpu.VMEM((2, 512, 128), F32),
        pltpu.VMEM((2, 25, 64, 256), BF),
        pltpu.VMEM((NSTEP, 8, 64, 256), BF),
        pltpu.VMEM((2, 8, 16, 128), BF),
        pltpu.VMEM((NSTEP, 512, 256), BF),
        pltpu.VMEM((2, 128, 128), BF),
        pltpu.VMEM((NSTEP, 4, CAP, 256), BF),
        pltpu.VMEM((2, 4, 80, 128), BF),
        pltpu.VMEM((2, 4, 2, 64, MCAP), F32),
        pltpu.VMEM((2, 4, 64, MCAP), F32),
        pltpu.VMEM((2, 2, 4, 4, 8, MCAP), F32),
        pltpu.VMEM((2, 2, 4, 8, MCAP), F32),
        pltpu.VMEM((2, 2, 3, 4, 8, MCAP), F32),
        pltpu.VMEM((2, 2, 3, 8, MCAP), F32),
        pltpu.VMEM((2, 2, 8, MCAP), F32),
        pltpu.VMEM((128, 128), F32),
        dma((4,)),
        dma((NSTEP, 3)), dma((NSTEP, 3)), dma((NSTEP,)),
        dma((2, 3)), dma((2, 3)), dma((2,)),
        dma((NSTEP, 7)), dma((NSTEP, 7)), dma((NSTEP,)),
        dma((2, 7)), dma((2, 7)), dma((2,)),
        dma((NSTEP, 2)), dma((NSTEP, 2)), dma((NSTEP, 2)), dma((NSTEP, 2)),
        dma((2, 2)), dma((2, 2)), dma((2,)), dma((2,)),
        dma((2,)), dma((2,)),
        dma((2, 6)), dma((2, 6)), dma((2, 6)), dma((2, 6)),
    ]
    return pl.pallas_call(
        kernel,
        out_shape=jax.ShapeDtypeStruct(OUT, F32),
        in_specs=[pl.BlockSpec(memory_space=pltpu.SMEM)] * 4 + [vmem] * 3 + [hbm, hbm],
        out_specs=vmem,
        scratch_shapes=scratch,
        compiler_params=pltpu.CompilerParams(
            collective_id=0, has_side_effects=True, vmem_limit_bytes=52 * 2**20
        ),
        name="cycle",
    )(occ_irrep, slab_occ, col_occ, occ_energy, virt_irrep.reshape(1, 1024), virt_energy.reshape(1, 1024),
      drive, amp, wraw)


def body(
    amplitudes,
    cycle_block,
    drive_term,
    occ_energy,
    virt_energy,
    occ_irrep,
    virt_irrep,
    slab_occ,
    col_occ,
):
    amp = amplitudes.reshape(25, 32, 1024)
    wraw = jnp.transpose(cycle_block, (1, 2, 0, 3)).reshape(3200, 1024)
    drive = jnp.transpose(drive_term, (0, 2, 1, 3)).reshape(32, 1024)
    half = (jnp.arange(1024, dtype=jnp.int32) // 16) % 2
    count = jnp.sum(virt_irrep * jnp.where(half == 0, 1, 4096))
    first, second = count % 4096, count // 4096
    fits = (
        (first <= CAP) & (first >= 512 - CAP) & (second <= CAP) & (second >= 512 - CAP)
        & (first + second <= MCAP) & (first + second >= 1024 - MCAP)
    )
    return lax.cond(
        fits, folded_update, general_update,
        amp, wraw, drive, occ_irrep, virt_irrep, slab_occ, col_occ, occ_energy, virt_energy,
    )


def solution(mesh):
    in_specs = (
        P(None, "occ", "virt", None),
        P("virt", None, "occ", None),
        P(None, "virt", "occ", None),
        P(),
        P(),
        P(),
        P(),
        P(),
        P(),
    )
    out_specs = P(None, "virt", "occ", None)
    return jax.shard_map(body, mesh=mesh, in_specs=in_specs, out_specs=out_specs, check_vma=False)
```

```python
import jax
import jax.numpy as jnp
from jax import lax
from jax.experimental import pallas as pl
from jax.experimental.pallas import tpu as pltpu
from jax.sharding import PartitionSpec as P

MESH = pl.DeviceIdType.MESH
CAP = 304
CAPL = 320
MCAP = 640
NSTEP = 6
OUT = (1, 32, 1, 1024)
GL = 1
BF = jnp.bfloat16
F32 = jnp.float32


def pick_entries(values_table, indices):
    hits = indices[:, None] == jnp.arange(values_table.shape[0], dtype=jnp.int32)[None, :]
    return jnp.sum(
        jnp.where(hits, values_table[None, :], jnp.zeros((), values_table.dtype)), axis=1
    )


def spread_all(block, axis, count):
    return lax.all_to_all(jnp.broadcast_to(block[None], (count,) + block.shape), axis, 0, 0, tiled=True)


def general_update(amp, wraw, drive, occ_irrep, virt_irrep, slab_occ, col_occ, occ_energy, virt_energy):
    x = lax.axis_index("occ")
    v = lax.axis_index("virt")
    slab_irrep = pick_entries(occ_irrep, slab_occ)[0]
    col_here = lax.dynamic_slice_in_dim(col_occ, x, 1)
    col_irrep = pick_entries(occ_irrep, col_here)[0]
    irr_k = lax.dynamic_slice_in_dim(occ_irrep, x * 25, 25)
    irr_a = lax.dynamic_slice_in_dim(virt_irrep, v * 32, 32)
    parity = slab_irrep + irr_k[:, None, None] + irr_a[None, :, None] + virt_irrep[None, None, :]
    masked = jnp.where(parity % 2 == 0, amp, jnp.zeros((), amp.dtype))
    pair_block = spread_all(masked, "occ", 4).reshape(100, 32, 1024)
    relaid = lax.all_to_all(pair_block, "virt", split_axis=2, concat_axis=1, tiled=True)
    w = wraw.reshape(100, 32, 1024)
    partial_value = jnp.einsum("kac,kcb->ab", relaid, w, preferred_element_type=F32)
    parts = lax.all_to_all(partial_value.reshape(32, 32, 1024), "virt", 0, 0, tiled=True)
    cycle_sum = jnp.sum(parts, axis=0)
    e_slab = pick_entries(occ_energy, slab_occ)[0]
    e_col = pick_entries(occ_energy, col_here)[0]
    e_rows = lax.dynamic_slice_in_dim(virt_energy, v * 32, 32)
    divisor = e_rows[:, None] + virt_energy[None, :] - e_slab - e_col
    out_parity = slab_irrep + irr_a[:, None] + col_irrep + virt_irrep[None, :]
    value = (drive.astype(F32) + cycle_sum) / divisor
    return jnp.where(out_parity % 2 == 0, value, jnp.zeros((), F32)).reshape(OUT)


def block_transpose(tiles, b1, b0):
    t = list(tiles)
    for q in (0, 1):
        a, b = t[q], t[q + 2]
        t[q] = jnp.where(b1, pltpu.roll(b, 64, 1), a)
        t[q + 2] = jnp.where(b1, b, pltpu.roll(a, 64, 1))
    for q in (0, 2):
        a, b = t[q], t[q + 1]
        t[q] = jnp.where(b0, pltpu.roll(b, 32, 1), a)
        t[q + 1] = jnp.where(b0, b, pltpu.roll(a, 96, 1))
    return t


def kernel(
    occ_ref, slab_ref, colo_ref, eocc_ref, virt_ref, evirt_ref, drive_ref, amp, wraw,
    out,
    wv, wf, wrep, wide, widel, amask, wmask, vrow, col, crow, rankb, rankh, fold, unfold, foldb, unfoldb, clsb, mbuf, sbuf, sleft, abuf, aleft,
    xbuf, xleft, zacc, crecv, tsum, t2, r1buf, r2buf, fin, ecol,
    wsem, ysend, yrecv, yloc, ysendl, yrecvl, ylocl,
    zsend, zrecv, zloc, zsendl, zrecvl, zlocl,
    xsend, xrecv, fsend, frecv, xsendl, xrecvl, fsendl, frecvl,
    csend, crecvs, r1send, r1recv, r2send, r2recv,
):
    x = lax.axis_index("occ")
    v = lax.axis_index("virt")
    y = v // 8
    z = (v // 2) % 4
    core = v % 2
    me8 = z * 2 + core

    def virt_at(yy, zz, cc):
        return (yy * 4 + zz) * 2 + cc

    right = (x + 1) % 4
    left = (x + 3) % 4

    def y_peer(o):
        return (x, virt_at((y + o) % 4, z, core))

    def z_peer(o):
        oz, oc = o // 2, o % 2
        return (x, virt_at(y, (z + oz) % 4, (core + oc) % 2))

    def z_slot(o):
        return ((z + o // 2) % 4) * 2 + (core + o % 2) % 2

    def remote(src, dst, ssem, rsem, dev):
        return pltpu.make_async_remote_copy(
            src_ref=src, dst_ref=dst, send_sem=ssem, recv_sem=rsem,
            device_id=dev, device_id_type=MESH,
        )

    def y_src(h, k0, nk, yd):
        return amp.at[pl.ds(k0, nk), pl.ds(16 * h, 16), pl.ds(pl.multiple_of(256 * yd, 256), 256)]

    def y_dst(h, k0, nk):
        return mbuf.at[h, pl.ds(k0, nk), pl.ds(pl.multiple_of(16 * y, 16), 16), :]

    def y_copy(n, o):
        h, g = n // 3, n % 3
        return remote(y_src(h, 8 * g, 8, (y + o) % 4), y_dst(h, 8 * g, 8),
                      ysend.at[n, o - 1], yrecv.at[n, o - 1], y_peer(o))

    def y_copyl(h, o):
        return remote(y_src(h, 24, 1, (y + o) % 4), y_dst(h, 24, 1),
                      ysendl.at[h, o - 1], yrecvl.at[h, o - 1], y_peer(o))

    def y_own(n):
        h, g = n // 3, n % 3
        return pltpu.make_async_copy(y_src(h, 8 * g, 8, y), y_dst(h, 8 * g, 8), yloc.at[n])

    def y_ownl(h):
        return pltpu.make_async_copy(y_src(h, 24, 1, y), y_dst(h, 24, 1), ylocl.at[h])

    def z_dst(n):
        return abuf.at[n, pl.ds(pl.multiple_of(64 * me8, 64), 64), :]

    def z_dstl(h):
        return aleft.at[h, pl.ds(pl.multiple_of(16 * me8, 16), 16), :]

    def z_copy(n, o):
        return remote(sbuf.at[n, z_slot(o)], z_dst(n), zsend.at[n, o - 1], zrecv.at[n, o - 1], z_peer(o))

    def z_copyl(h, o):
        return remote(sleft.at[h, z_slot(o)], z_dstl(h), zsendl.at[h, o - 1], zrecvl.at[h, o - 1], z_peer(o))

    def z_own(n):
        return pltpu.make_async_copy(sbuf.at[n, me8], z_dst(n), zloc.at[n])

    def z_ownl(h):
        return pltpu.make_async_copy(sleft.at[h, me8], z_dstl(h), zlocl.at[h])

    def x_copy(n, side):
        return remote(xbuf.at[n, 0], xbuf.at[n, 1 + side], xsend.at[n, side], xrecv.at[n, side],
                      ((right, left)[side], v))

    def f_copy(n, side):
        lanes = pl.ds(128 * side, 128)
        return remote(xbuf.at[n, 1 + side, :, lanes], xbuf.at[n, 3, :, lanes],
                      fsend.at[n, side], frecv.at[n, side], ((right, left)[side], v))

    def x_copyl(h, side):
        return remote(xleft.at[h, 0], xleft.at[h, 1 + side], xsendl.at[h, side], xrecvl.at[h, side],
                      ((right, left)[side], v))

    def f_copyl(h, side):
        return remote(xleft.at[h, 1 + side], xleft.at[h, 3], fsendl.at[h], frecvl.at[h],
                      ((right, left)[side], v))

    def c_copy(h):
        return remote(zacc.at[h, :, 1 - core], crecv.at[h], csend.at[h], crecvs.at[h],
                      (x, virt_at(y, z, 1 - core)))

    def r1_copy(h, axis, o):
        if axis == 0:
            yd = (y + o) % 4
            return remote(tsum.at[h, 0, :, yd], r1buf.at[h, 0, o - 1], r1send.at[h, o - 1],
                          r1recv.at[h, o - 1], (x, virt_at(yd, z, core)))
        zd = (z + o) % 4
        return remote(tsum.at[h, 1, zd], r1buf.at[h, 1, o - 1], r1send.at[h, 2 + o],
                      r1recv.at[h, 2 + o], (x, virt_at(y, zd, core)))

    def r2_copy(h, axis, o):
        if axis == 0:
            zd = (z + o) % 4
            return remote(t2.at[h, 0, zd], r2buf.at[h, 0, o - 1], r2send.at[h, o - 1],
                          r2recv.at[h, o - 1], (x, virt_at(y, zd, core)))
        yd = (y + o) % 4
        return remote(t2.at[h, 1, yd], r2buf.at[h, 1, o - 1], r2send.at[h, 2 + o],
                      r2recv.at[h, 2 + o], (x, virt_at(yd, z, core)))

    barrier = pltpu.get_barrier_semaphore()
    peers = [y_peer(o) for o in (1, 2, 3)] + [z_peer(o) for o in range(1, 8)] + [(right, v), (left, v)]
    for dev in peers:
        pl.semaphore_signal(barrier, inc=1, device_id=dev, device_id_type=MESH)
    pl.semaphore_wait(barrier, len(peers))

    def w_copy(i):
        rows = pl.ds(800 * i, 800)
        return pltpu.make_async_copy(wraw.at[rows], wv.at[rows], wsem.at[i])

    for n in range(NSTEP):
        for o in (2, 1, 3):
            y_copy(n, o).start()
        y_own(n).start()
        if n % 3 == GL:
            for o in (2, 1, 3):
                y_copyl(n // 3, o).start()
            y_ownl(n // 3).start()
        if n == 1:
            for i in range(4):
                w_copy(i).start()

    lane128 = lax.broadcasted_iota(jnp.int32, (1, 128), 1)

    slab = slab_ref[0]
    slab_irr = occ_ref[slab]
    colo = colo_ref[x]
    col_irr = occ_ref[colo]

    def flip(row, par):
        return jnp.where(par % 2 == 1, 1.0 - row, row)

    def one_hot(cond):
        return cond.astype(F32).astype(BF)

    vrow[...] = virt_ref[...].astype(F32)
    col[...] = jnp.transpose(jnp.broadcast_to(vrow[...], (128, 1024)))
    for h in range(2):
        rows = jnp.concatenate(
            [col[pl.ds(pl.multiple_of(256 * yy + 32 * (me8) + 16 * h, 16), 16), :] for yy in range(4)], axis=0)
        for t in range(2):
            c_mid = vrow[:, pl.ds(pl.multiple_of(256 * y + 128 * t, 128), 128)]
            for par in range(2):
                amask[h, par, :, 128 * t:128 * t + 128] = one_hot(rows == flip(c_mid, slab_irr + par))

    def rank_tables():
        def chunk(i, carry):
            rows = lax.broadcasted_iota(jnp.int32, (128, 1024), 0) + 128 * i
            cols = lax.broadcasted_iota(jnp.int32, (128, 1024), 1)
            before = cols < rows
            ones = col[...].astype(BF)
            count = jnp.dot(one_hot(before), ones, preferred_element_type=F32)
            same = ((rows ^ cols) & 16) == 0
            count_h = jnp.dot(one_hot(before & same), ones, preferred_element_type=F32)
            here = pl.ds(pl.multiple_of(128 * i, 128), 128)
            cls = col[here, :]
            rows = lax.broadcasted_iota(jnp.int32, (128, 128), 0) + 128 * i
            rankb[here, :] = jnp.where(cls == 1.0, count, rows.astype(F32) - count)
            rows_h = (rows >> 5) * 16 + (rows & 15)
            count_h = jnp.where(cls == 1.0, count_h, rows_h.astype(F32) - count_h)
            for b in range(8):
                place = (((i % 2) * 4 + b // 2) * 4 + i // 2) * 16
                rankh[b % 2, pl.ds(pl.multiple_of(place, 16), 16), :] = count_h[16 * b:16 * b + 16]
                clsb[b % 2, pl.ds(pl.multiple_of(place, 16), 16), :] = cls[16 * b:16 * b + 16]
            return carry

        lax.fori_loop(0, 8, chunk, 0)
        for h in range(2):
            row = jnp.transpose(rankh[h])[0:1]
            fold[h] = one_hot(lax.broadcasted_iota(jnp.int32, (CAPL, 512), 0).astype(F32) == row)

    def more_tables():
        for h in range(2):
            for t in range(3):
                w = min(128, CAPL - 128 * t)
                lane = lax.broadcasted_iota(jnp.int32, (512, w), 1).astype(F32) + 128.0 * t
                unfold[h, :, 128 * t:128 * t + w] = one_hot(rankh[h][:, :w] == lane)
        for t in range(MCAP // 128):
            lane = lax.broadcasted_iota(jnp.int32, (1024, 128), 1).astype(F32) + 128.0 * t
            foldb[:, 128 * t:128 * t + 128] = one_hot(rankb[...] == lane)
        crows = col[pl.ds(pl.multiple_of(32 * v, 32), 32), :]
        for par in range(2):
            for t in range(8):
                row = flip(vrow[:, 128 * t:128 * t + 128], col_irr + par)
                wmask[par, :, 128 * t:128 * t + 128] = one_hot(crows == row)
        sub = lax.broadcasted_iota(jnp.int32, (32, 128), 0)
        hit = sub == lax.broadcasted_iota(jnp.int32, (32, 128), 1) % 32
        crow[...] = jnp.sum(jnp.where(hit, crows, 0.0), axis=0, keepdims=True)

    def last_tables():
        row = jnp.transpose(rankb[...])[0:1]
        unfoldb[...] = one_hot(lax.broadcasted_iota(jnp.int32, (MCAP, 1024), 0).astype(F32) == row)

    def lane_class(src, k0, step):
        row = flip(crow[...], slab_irr + occ_ref[25 * src + k0])
        for q in range(1, 4):
            other = flip(crow[...], slab_irr + occ_ref[25 * src + k0 + q * step])
            row = jnp.where(lane128 // 32 == q, other, row)
        return row

    def prepare_w(i):
        w_copy(i).wait()

        def mask_k(k, carry):
            rows = pl.ds(pl.multiple_of(800 * i + 32 * k, 32), 32)
            wv[rows, :] = wv[rows, :] * wmask[occ_ref[25 * i + k]]
            return carry

        lax.fori_loop(0, 25, mask_k, 0, unroll=5)
        rows = pl.ds(pl.multiple_of(800 * i, 32), 800)
        value = jnp.dot(wv[rows, :], foldb[...], preferred_element_type=F32).astype(BF)
        for g in range(3):
            wf[g, i] = value[256 * g:256 * g + 256]
        for q in range(4):
            wrep[i, q] = value[768:800]

    rank_tables()
    more_tables()

    def relay(n):
        h, g = n // 3, n % 3
        for o in (1, 2, 3):
            y_copy(n, o).wait_recv()
        y_own(n).wait()
        b1 = (lane128 // 64) % 2 == 1
        b0 = (lane128 // 32) % 2 == 1
        for kg in range(2):
            rowsq = []
            for q in range(4):
                k = 8 * g + 4 * kg + q
                par = occ_ref[25 * x + k]
                rowsq.append((mbuf[h, k] * amask[h, par]).astype(F32))
            for t in range(2):
                res = block_transpose([r[:, 128 * t:128 * t + 128] for r in rowsq], b1, b0)
                for d in range(4):
                    sbuf[n, 4 * t + d, :, 128 * kg:128 * kg + 128] = res[d].astype(BF)
        for o in (4, 5, 2, 3, 6, 7, 1):
            z_copy(n, o).start()
        z_own(n).start()

        @pl.when(g == GL)
        def _():
            for o in (1, 2, 3):
                y_copyl(h, o).wait_recv()
            y_ownl(h).wait()
            par = occ_ref[25 * x + 24]
            whole = (mbuf[h, 24] * amask[h, par]).astype(F32)
            for t in range(2):
                res = block_transpose(
                    [whole[16 * q:16 * q + 16, 128 * t:128 * t + 128] for q in range(4)], b1, b0)
                for d in range(4):
                    sleft[h, 4 * t + d] = res[d].astype(BF)
            for o in (4, 5, 2, 3, 6, 7, 1):
                z_copyl(h, o).start()
            z_ownl(h).start()

    def fold_step(n):
        h, g = n // 3, n % 3
        for o in range(1, 8):
            z_copy(n, o).wait_recv()
        z_own(n).wait()
        xbuf[n, 0] = jnp.dot(fold[h, :CAP], abuf[n], preferred_element_type=F32).astype(BF)
        for side in range(2):
            x_copy(n, side).start()

        @pl.when(g == GL)
        def _():
            for o in range(1, 8):
                z_copyl(h, o).wait_recv()
            z_ownl(h).wait()
            got = aleft[h].astype(F32)
            parts = []
            for s in range(8):
                for q in range(4):
                    parts.append(jnp.where(lane128 // 32 == q, got[16 * s:16 * s + 16], 0.0))
            spread = jnp.concatenate(parts, axis=0).astype(BF)
            both = jnp.dot(fold[h], spread, preferred_element_type=F32)
            both = both + pltpu.roll(both, 64, 1)
            both = both + pltpu.roll(both, 32, 1)
            packed = both[0:80]
            for q in range(1, 4):
                packed = jnp.where(lane128 // 32 == q, both[80 * q:80 * q + 80], packed)
            xleft[h, 0] = packed.astype(BF)
            for side in range(2):
                x_copyl(h, side).start()

    def spread(n, slot):
        h, g = n // 3, n % 3
        src = (x + (0, 3, 1, 2)[slot]) % 4
        part = jnp.dot(unfold[h, :, :CAP], xbuf[n, slot], preferred_element_type=F32)
        cls = clsb[h]
        for t in range(2):
            piece = jnp.where(
                cls == lane_class(src, 8 * g + 4 * t, 1), part[:, 128 * t:128 * t + 128], 0.0).astype(BF)
            for i in range(8):
                wide[n % 2, i // 2, i % 2, :, pl.ds(pl.multiple_of(256 * src + 128 * t, 128), 128)] = (
                    piece[64 * i:64 * i + 64])

    def spread_left(h, slot):
        src = (x + (0, 3, 1, 2)[slot]) % 4
        got = xleft[h, slot].astype(F32)
        stacked = jnp.concatenate(
            [jnp.where(lane128 // 32 == q, got, 0.0) for q in range(4)], axis=0).astype(BF)
        part = jnp.dot(unfold[h], stacked, preferred_element_type=F32)
        part = jnp.where(clsb[h] == lane_class(src, 24, 0), part, 0.0).astype(BF)
        for i in range(8):
            widel[h, i // 2, i % 2, :, pl.ds(pl.multiple_of(128 * src, 128), 128)] = part[64 * i:64 * i + 64]

    def near_step(n):
        h, g = n // 3, n % 3
        for side in range(2):
            x_copy(n, side).wait_recv()
            f_copy(n, side).start()

        @pl.when(g == GL)
        def _():
            for side in range(2):
                x_copyl(h, side).wait_recv()

            @pl.when(h == 0)
            def _():
                f_copyl(h, 0).start()

            @pl.when(h == 1)
            def _():
                f_copyl(h, 1).start()

        for slot in range(3):
            spread(n, slot)

        @pl.when(g == GL)
        def _():
            for slot in range(3):
                spread_left(h, slot)

    def product(n, cc):
        h, g = n // 3, n % 3
        left_side = wide[n % 2, :, cc].reshape(256, 1024)
        value = jnp.dot(left_side, wf[g].reshape(1024, MCAP), preferred_element_type=F32).reshape(4, 64, MCAP)

        @pl.when(g == 0)
        def _():
            zacc[h, :, cc] = value

        @pl.when(g > 0)
        def _():
            zacc[h, :, cc] += value

    def far_step(n):
        h, g = n // 3, n % 3
        for side in range(2):
            f_copy(n, side).wait_recv()
        spread(n, 3)
        product(n, 1 - core)

        @pl.when(g == 2)
        def _():
            c_copy(h).start()

        product(n, core)

        @pl.when(g == GL)
        def _():
            f_copyl(h, 0).wait_recv()
            spread_left(h, 3)
            table = wrep[...].reshape(512, MCAP)
            for cc in range(2):
                zacc[h, :, cc] += jnp.dot(
                    widel[h, :, cc].reshape(256, 512), table, preferred_element_type=F32).reshape(4, 64, MCAP)

    def sum_core(h):
        c_copy(h).wait_recv()
        for zz in range(4):
            both = zacc[h, zz, core] + crecv[h, zz]
            for yy in range(4):
                for rh in range(2):
                    r0 = yy * 16 + rh * 8
                    tsum[h, rh, zz, yy] = both[r0:r0 + 8]
        for axis in range(2):
            for o in (2, 1, 3):
                r1_copy(h, axis, o).start()

    def sum_first(h):
        for axis in range(2):
            for o in (1, 2, 3):
                r1_copy(h, axis, o).wait_recv()
        for i in range(4):
            t2[h, 0, i] = tsum[h, 0, i, y] + r1buf[h, 0, 0, i] + r1buf[h, 0, 1, i] + r1buf[h, 0, 2, i]
            t2[h, 1, i] = tsum[h, 1, z, i] + r1buf[h, 1, 0, i] + r1buf[h, 1, 1, i] + r1buf[h, 1, 2, i]
        for axis in range(2):
            for o in (2, 1, 3):
                r2_copy(h, axis, o).start()

    def sum_second(h):
        for axis in range(2):
            for o in (1, 2, 3):
                r2_copy(h, axis, o).wait_recv()
        fin[h, 0] = t2[h, 0, z] + r2buf[h, 0, 0] + r2buf[h, 0, 1] + r2buf[h, 0, 2]
        fin[h, 1] = t2[h, 1, y] + r2buf[h, 1, 0] + r2buf[h, 1, 1] + r2buf[h, 1, 2]

    def step(n, carry):
        @pl.when(n < NSTEP)
        def _():
            relay(n)

        @pl.when(n == 0)
        def _():
            prepare_w(0)
            prepare_w(1)

        @pl.when(jnp.logical_and(n >= 1, n < NSTEP + 1))
        def _():
            fold_step(n - 1)

        @pl.when(n == 1)
        def _():
            prepare_w(2)
            prepare_w(3)

        @pl.when(n == 3)
        def _():
            last_tables()

        @pl.when(jnp.logical_and(n >= 2, n < NSTEP + 2))
        def _():
            near_step(n - 2)

        @pl.when(jnp.logical_or(n == 6, n == 9))
        def _():
            sum_core(n // 3 - 2)

        @pl.when(jnp.logical_or(n == 7, n == 10))
        def _():
            sum_first(n // 3 - 2)

        @pl.when(jnp.logical_and(n >= 3, n < NSTEP + 3))
        def _():
            far_step(n - 3)

        return carry

    lax.fori_loop(0, 11, step, 0)
    sum_second(0)
    sum_second(1)

    total = jnp.concatenate([fin[0, 0], fin[0, 1], fin[1, 0], fin[1, 1]], axis=0)
    hi = total.astype(BF)
    rest = total - hi.astype(F32)
    mid = rest.astype(BF)
    low = (rest - mid.astype(F32)).astype(BF)
    tile = evirt_ref[:, pl.ds(pl.multiple_of(128 * (v // 4), 128), 128)]
    e_rows = jnp.transpose(jnp.broadcast_to(tile, (128, 128)))
    ecol[...] = e_rows
    e_here = ecol[pl.ds(pl.multiple_of(32 * (v % 4), 32), 32), :]
    e_slab = eocc_ref[slab]
    e_col = eocc_ref[colo]
    cls = col[pl.ds(pl.multiple_of(32 * v, 32), 32), :]
    for t in range(8):
        lanes = slice(128 * t, 128 * t + 128)
        table = unfoldb[:, lanes]
        cycle_sum = (
            jnp.dot(hi, table, preferred_element_type=F32)
            + jnp.dot(mid, table, preferred_element_type=F32)
        ) + jnp.dot(low, table, preferred_element_type=F32)
        divisor = e_here + evirt_ref[:, lanes] - e_slab - e_col
        value = (drive_ref[:, lanes].astype(F32) + cycle_sum) / divisor
        out[0, :, 0, lanes] = jnp.where(cls == flip(vrow[:, lanes], slab_irr + col_irr), value, 0.0)

    def finish(n, carry):
        for o in (1, 2, 3):
            y_copy(n, o).wait_send()
        for o in range(1, 8):
            z_copy(n, o).wait_send()
        for side in range(2):
            x_copy(n, side).wait_send()
            f_copy(n, side).wait_send()
        return carry

    lax.fori_loop(0, NSTEP, finish, 0)

    def finish_half(h, carry):
        for o in (1, 2, 3):
            y_copyl(h, o).wait_send()
        for o in range(1, 8):
            z_copyl(h, o).wait_send()
        for side in range(2):
            x_copyl(h, side).wait_send()
        f_copyl(h, 0).wait_send()
        c_copy(h).wait_send()
        for axis in range(2):
            for o in (1, 2, 3):
                r1_copy(h, axis, o).wait_send()
                r2_copy(h, axis, o).wait_send()
        return carry

    lax.fori_loop(0, 2, finish_half, 0)


def folded_update(amp, wraw, drive, occ_irrep, virt_irrep, slab_occ, col_occ, occ_energy, virt_energy):
    dma = pltpu.SemaphoreType.DMA
    vmem = pl.BlockSpec(memory_space=pltpu.VMEM)
    hbm = pl.BlockSpec(memory_space=pl.ANY)
    scratch = [
        pltpu.VMEM((3200, 1024), BF),
        pltpu.VMEM((3, 4, 256, MCAP), BF),
        pltpu.VMEM((4, 4, 32, MCAP), BF),
        pltpu.VMEM((2, 4, 2, 64, 1024), BF),
        pltpu.VMEM((2, 4, 2, 64, 512), BF),
        pltpu.VMEM((2, 2, 64, 256), BF),
        pltpu.VMEM((2, 32, 1024), BF),
        pltpu.VMEM((1, 1024), F32),
        pltpu.VMEM((1024, 128), F32),
        pltpu.VMEM((1, 128), F32),
        pltpu.VMEM((1024, 128), F32),
        pltpu.VMEM((2, 512, 128), F32),
        pltpu.VMEM((2, CAPL, 512), BF),
        pltpu.VMEM((2, 512, CAPL), BF),
        pltpu.VMEM((1024, MCAP), BF),
        pltpu.VMEM((MCAP, 1024), BF),
        pltpu.VMEM((2, 512, 128), F32),
        pltpu.VMEM((2, 25, 64, 256), BF),
        pltpu.VMEM((NSTEP, 8, 64, 256), BF),
        pltpu.VMEM((2, 8, 16, 128), BF),
        pltpu.VMEM((NSTEP, 512, 256), BF),
        pltpu.VMEM((2, 128, 128), BF),
        pltpu.VMEM((NSTEP, 4, CAP, 256), BF),
        pltpu.VMEM((2, 4, 80, 128), BF),
        pltpu.VMEM((2, 4, 2, 64, MCAP), F32),
        pltpu.VMEM((2, 4, 64, MCAP), F32),
        pltpu.VMEM((2, 2, 4, 4, 8, MCAP), F32),
        pltpu.VMEM((2, 2, 4, 8, MCAP), F32),
        pltpu.VMEM((2, 2, 3, 4, 8, MCAP), F32),
        pltpu.VMEM((2, 2, 3, 8, MCAP), F32),
        pltpu.VMEM((2, 2, 8, MCAP), F32),
        pltpu.VMEM((128, 128), F32),
        dma((4,)),
        dma((NSTEP, 3)), dma((NSTEP, 3)), dma((NSTEP,)),
        dma((2, 3)), dma((2, 3)), dma((2,)),
        dma((NSTEP, 7)), dma((NSTEP, 7)), dma((NSTEP,)),
        dma((2, 7)), dma((2, 7)), dma((2,)),
        dma((NSTEP, 2)), dma((NSTEP, 2)), dma((NSTEP, 2)), dma((NSTEP, 2)),
        dma((2, 2)), dma((2, 2)), dma((2,)), dma((2,)),
        dma((2,)), dma((2,)),
        dma((2, 6)), dma((2, 6)), dma((2, 6)), dma((2, 6)),
    ]
    return pl.pallas_call(
        kernel,
        out_shape=jax.ShapeDtypeStruct(OUT, F32),
        in_specs=[pl.BlockSpec(memory_space=pltpu.SMEM)] * 4 + [vmem] * 3 + [hbm, hbm],
        out_specs=vmem,
        scratch_shapes=scratch,
        compiler_params=pltpu.CompilerParams(
            collective_id=0, has_side_effects=True, vmem_limit_bytes=52 * 2**20
        ),
        name="cycle",
    )(occ_irrep, slab_occ, col_occ, occ_energy, virt_irrep.reshape(1, 1024), virt_energy.reshape(1, 1024),
      drive, amp, wraw)


def body(
    amplitudes,
    cycle_block,
    drive_term,
    occ_energy,
    virt_energy,
    occ_irrep,
    virt_irrep,
    slab_occ,
    col_occ,
):
    amp = amplitudes.reshape(25, 32, 1024)
    wraw = jnp.transpose(cycle_block, (1, 2, 0, 3)).reshape(3200, 1024)
    drive = jnp.transpose(drive_term, (0, 2, 1, 3)).reshape(32, 1024)
    half = (jnp.arange(1024, dtype=jnp.int32) // 16) % 2
    count = jnp.sum(virt_irrep * jnp.where(half == 0, 1, 4096))
    first, second = count % 4096, count // 4096
    fits = (
        (first <= CAP) & (first >= 512 - CAP) & (second <= CAP) & (second >= 512 - CAP)
        & (first + second <= MCAP) & (first + second >= 1024 - MCAP)
    )
    return lax.cond(
        fits, folded_update, general_update,
        amp, wraw, drive, occ_irrep, virt_irrep, slab_occ, col_occ, occ_energy, virt_energy,
    )


def solution(mesh):
    in_specs = (
        P(None, "occ", "virt", None),
        P("virt", None, "occ", None),
        P(None, "virt", "occ", None),
        P(),
        P(),
        P(),
        P(),
        P(),
        P(),
    )
    out_specs = P(None, "virt", "occ", None)
    return jax.shard_map(body, mesh=mesh, in_specs=in_specs, out_specs=out_specs, check_vma=False)
```

```python
import jax
import jax.numpy as jnp
from jax import lax
from jax.experimental import pallas as pl
from jax.experimental.pallas import tpu as pltpu
from jax.sharding import PartitionSpec as P

MESH = pl.DeviceIdType.MESH
CAP = 304
CAPL = 320
MCAP = 640
NSTEP = 6
OUT = (1, 32, 1, 1024)
GL = 1
BF = jnp.bfloat16
F32 = jnp.float32


def pick_entries(values_table, indices):
    hits = indices[:, None] == jnp.arange(values_table.shape[0], dtype=jnp.int32)[None, :]
    return jnp.sum(
        jnp.where(hits, values_table[None, :], jnp.zeros((), values_table.dtype)), axis=1
    )


def spread_all(block, axis, count):
    return lax.all_to_all(jnp.broadcast_to(block[None], (count,) + block.shape), axis, 0, 0, tiled=True)


def general_update(amp, wraw, drive, occ_irrep, virt_irrep, slab_occ, col_occ, occ_energy, virt_energy):
    x = lax.axis_index("occ")
    v = lax.axis_index("virt")
    slab_irrep = pick_entries(occ_irrep, slab_occ)[0]
    col_here = lax.dynamic_slice_in_dim(col_occ, x, 1)
    col_irrep = pick_entries(occ_irrep, col_here)[0]
    irr_k = lax.dynamic_slice_in_dim(occ_irrep, x * 25, 25)
    irr_a = lax.dynamic_slice_in_dim(virt_irrep, v * 32, 32)
    parity = slab_irrep + irr_k[:, None, None] + irr_a[None, :, None] + virt_irrep[None, None, :]
    masked = jnp.where(parity % 2 == 0, amp, jnp.zeros((), amp.dtype))
    pair_block = spread_all(masked, "occ", 4).reshape(100, 32, 1024)
    relaid = lax.all_to_all(pair_block, "virt", split_axis=2, concat_axis=1, tiled=True)
    w = wraw.reshape(100, 32, 1024)
    partial_value = jnp.einsum("kac,kcb->ab", relaid, w, preferred_element_type=F32)
    parts = lax.all_to_all(partial_value.reshape(32, 32, 1024), "virt", 0, 0, tiled=True)
    cycle_sum = jnp.sum(parts, axis=0)
    e_slab = pick_entries(occ_energy, slab_occ)[0]
    e_col = pick_entries(occ_energy, col_here)[0]
    e_rows = lax.dynamic_slice_in_dim(virt_energy, v * 32, 32)
    divisor = e_rows[:, None] + virt_energy[None, :] - e_slab - e_col
    out_parity = slab_irrep + irr_a[:, None] + col_irrep + virt_irrep[None, :]
    value = (drive.astype(F32) + cycle_sum) / divisor
    return jnp.where(out_parity % 2 == 0, value, jnp.zeros((), F32)).reshape(OUT)


def block_transpose(tiles, b1, b0):
    t = list(tiles)
    for q in (0, 1):
        a, b = t[q], t[q + 2]
        t[q] = jnp.where(b1, pltpu.roll(b, 64, 1), a)
        t[q + 2] = jnp.where(b1, b, pltpu.roll(a, 64, 1))
    for q in (0, 2):
        a, b = t[q], t[q + 1]
        t[q] = jnp.where(b0, pltpu.roll(b, 32, 1), a)
        t[q + 1] = jnp.where(b0, b, pltpu.roll(a, 96, 1))
    return t


def kernel(
    occ_in, slab_in, colo_in, eocc_in, virt_in, evirt_in, drive_in, amp, wraw,
    out, fits_ref,
    occ_ref, slab_ref, colo_ref, eocc_ref, virt_ref, evirt_ref, drive_ref,
    wv, wf, wrep, wide, widel, amask, wmask, vrow, col, crow, rankb, rankh, fold, unfold, foldb, unfoldb, clsb, mbuf, sbuf, sleft, abuf, aleft,
    xbuf, xleft, zacc, crecv, tsum, t2, r1buf, r2buf, fin, ecol,
    insem, wsem, ysend, yrecv, yloc, ysendl, yrecvl, ylocl,
    zsend, zrecv, zloc, zsendl, zrecvl, zlocl,
    xsend, xrecv, fsend, frecv, xsendl, xrecvl, fsendl, frecvl,
    csend, crecvs, r1send, r1recv, r2send, r2recv,
):
    x = lax.axis_index("occ")
    v = lax.axis_index("virt")
    y = v // 8
    z = (v // 2) % 4
    core = v % 2
    me8 = z * 2 + core

    def virt_at(yy, zz, cc):
        return (yy * 4 + zz) * 2 + cc

    right = (x + 1) % 4
    left = (x + 3) % 4

    def y_peer(o):
        return (x, virt_at((y + o) % 4, z, core))

    def z_peer(o):
        oz, oc = o // 2, o % 2
        return (x, virt_at(y, (z + oz) % 4, (core + oc) % 2))

    def z_slot(o):
        return ((z + o // 2) % 4) * 2 + (core + o % 2) % 2

    def remote(src, dst, ssem, rsem, dev):
        return pltpu.make_async_remote_copy(
            src_ref=src, dst_ref=dst, send_sem=ssem, recv_sem=rsem,
            device_id=dev, device_id_type=MESH,
        )

    def y_src(h, k0, nk, yd):
        return amp.at[pl.ds(k0, nk), pl.ds(16 * h, 16), pl.ds(pl.multiple_of(256 * yd, 256), 256)]

    def y_dst(h, k0, nk):
        return mbuf.at[h, pl.ds(k0, nk), pl.ds(pl.multiple_of(16 * y, 16), 16), :]

    def y_copy(n, o):
        h, g = n // 3, n % 3
        return remote(y_src(h, 8 * g, 8, (y + o) % 4), y_dst(h, 8 * g, 8),
                      ysend.at[n, o - 1], yrecv.at[n, o - 1], y_peer(o))

    def y_copyl(h, o):
        return remote(y_src(h, 24, 1, (y + o) % 4), y_dst(h, 24, 1),
                      ysendl.at[h, o - 1], yrecvl.at[h, o - 1], y_peer(o))

    def y_own(n):
        h, g = n // 3, n % 3
        return pltpu.make_async_copy(y_src(h, 8 * g, 8, y), y_dst(h, 8 * g, 8), yloc.at[n])

    def y_ownl(h):
        return pltpu.make_async_copy(y_src(h, 24, 1, y), y_dst(h, 24, 1), ylocl.at[h])

    def z_dst(n):
        return abuf.at[n, pl.ds(pl.multiple_of(64 * me8, 64), 64), :]

    def z_dstl(h):
        return aleft.at[h, pl.ds(pl.multiple_of(16 * me8, 16), 16), :]

    def z_copy(n, o):
        return remote(sbuf.at[n, z_slot(o)], z_dst(n), zsend.at[n, o - 1], zrecv.at[n, o - 1], z_peer(o))

    def z_copyl(h, o):
        return remote(sleft.at[h, z_slot(o)], z_dstl(h), zsendl.at[h, o - 1], zrecvl.at[h, o - 1], z_peer(o))

    def z_own(n):
        return pltpu.make_async_copy(sbuf.at[n, me8], z_dst(n), zloc.at[n])

    def z_ownl(h):
        return pltpu.make_async_copy(sleft.at[h, me8], z_dstl(h), zlocl.at[h])

    def x_copy(n, side):
        return remote(xbuf.at[n, 0], xbuf.at[n, 1 + side], xsend.at[n, side], xrecv.at[n, side],
                      ((right, left)[side], v))

    def f_copy(n, side):
        lanes = pl.ds(128 * side, 128)
        return remote(xbuf.at[n, 1 + side, :, lanes], xbuf.at[n, 3, :, lanes],
                      fsend.at[n, side], frecv.at[n, side], ((right, left)[side], v))

    def x_copyl(h, side):
        return remote(xleft.at[h, 0], xleft.at[h, 1 + side], xsendl.at[h, side], xrecvl.at[h, side],
                      ((right, left)[side], v))

    def f_copyl(h, side):
        return remote(xleft.at[h, 1 + side], xleft.at[h, 3], fsendl.at[h], frecvl.at[h],
                      ((right, left)[side], v))

    def c_copy(h):
        return remote(zacc.at[h, :, 1 - core], crecv.at[h], csend.at[h], crecvs.at[h],
                      (x, virt_at(y, z, 1 - core)))

    def r1_copy(h, axis, o):
        if axis == 0:
            yd = (y + o) % 4
            return remote(tsum.at[h, 0, :, yd], r1buf.at[h, 0, o - 1], r1send.at[h, o - 1],
                          r1recv.at[h, o - 1], (x, virt_at(yd, z, core)))
        zd = (z + o) % 4
        return remote(tsum.at[h, 1, zd], r1buf.at[h, 1, o - 1], r1send.at[h, 2 + o],
                      r1recv.at[h, 2 + o], (x, virt_at(y, zd, core)))

    def r2_copy(h, axis, o):
        if axis == 0:
            zd = (z + o) % 4
            return remote(t2.at[h, 0, zd], r2buf.at[h, 0, o - 1], r2send.at[h, o - 1],
                          r2recv.at[h, o - 1], (x, virt_at(y, zd, core)))
        yd = (y + o) % 4
        return remote(t2.at[h, 1, yd], r2buf.at[h, 1, o - 1], r2send.at[h, 2 + o],
                      r2recv.at[h, 2 + o], (x, virt_at(yd, z, core)))

    loads = [
        pltpu.make_async_copy(src, dst, insem.at[i])
        for i, (src, dst) in enumerate((
            (occ_in, occ_ref), (slab_in, slab_ref), (colo_in, colo_ref), (eocc_in, eocc_ref),
            (virt_in, virt_ref), (evirt_in, evirt_ref), (drive_in, drive_ref)))
    ]
    for load in loads:
        load.start()

    barrier = pltpu.get_barrier_semaphore()
    peers = [y_peer(o) for o in (1, 2, 3)] + [z_peer(o) for o in range(1, 8)] + [(right, v), (left, v)]
    for dev in peers:
        pl.semaphore_signal(barrier, inc=1, device_id=dev, device_id_type=MESH)
    pl.semaphore_wait(barrier, len(peers))

    def w_copy(i):
        rows = pl.ds(800 * i, 800)
        return pltpu.make_async_copy(wraw.at[rows], wv.at[rows], wsem.at[i])

    for n in range(NSTEP):
        for o in (2, 1, 3):
            y_copy(n, o).start()
        y_own(n).start()
        if n % 3 == GL:
            for o in (2, 1, 3):
                y_copyl(n // 3, o).start()
            y_ownl(n // 3).start()
        if n == 1:
            for i in range(4):
                w_copy(i).start()

    lane128 = lax.broadcasted_iota(jnp.int32, (1, 128), 1)

    for load in loads:
        load.wait()
    slab = slab_ref[0]
    slab_irr = occ_ref[slab]
    colo = colo_ref[x]
    col_irr = occ_ref[colo]

    def flip(row, par):
        return jnp.where(par % 2 == 1, 1.0 - row, row)

    def one_hot(cond):
        return cond.astype(F32).astype(BF)

    vrow[...] = virt_ref[...].astype(F32)
    col[...] = jnp.transpose(jnp.broadcast_to(vrow[...], (128, 1024)))
    second = (lax.broadcasted_iota(jnp.int32, (1, 1024), 1) & 16) != 0
    ones_b = jnp.sum(jnp.where(second, vrow[...], 0.0))
    ones_a = jnp.sum(vrow[...]) - ones_b
    total = ones_a + ones_b
    fits = (
        (ones_a <= CAP) & (ones_a >= 512 - CAP) & (ones_b <= CAP) & (ones_b >= 512 - CAP)
        & (total <= MCAP) & (total >= 1024 - MCAP)
    )
    fits_ref[0] = fits.astype(jnp.int32)
    for h in range(2):
        rows = jnp.concatenate(
            [col[pl.ds(pl.multiple_of(256 * yy + 32 * (me8) + 16 * h, 16), 16), :] for yy in range(4)], axis=0)
        for t in range(2):
            c_mid = vrow[:, pl.ds(pl.multiple_of(256 * y + 128 * t, 128), 128)]
            for par in range(2):
                amask[h, par, :, 128 * t:128 * t + 128] = one_hot(rows == flip(c_mid, slab_irr + par))

    def rank_tables():
        def chunk(i, carry):
            rows = lax.broadcasted_iota(jnp.int32, (128, 1024), 0) + 128 * i
            cols = lax.broadcasted_iota(jnp.int32, (128, 1024), 1)
            before = cols < rows
            ones = col[...].astype(BF)
            count = jnp.dot(one_hot(before), ones, preferred_element_type=F32)
            same = ((rows ^ cols) & 16) == 0
            count_h = jnp.dot(one_hot(before & same), ones, preferred_element_type=F32)
            here = pl.ds(pl.multiple_of(128 * i, 128), 128)
            cls = col[here, :]
            rows = lax.broadcasted_iota(jnp.int32, (128, 128), 0) + 128 * i
            rankb[here, :] = jnp.where(cls == 1.0, count, rows.astype(F32) - count)
            rows_h = (rows >> 5) * 16 + (rows & 15)
            count_h = jnp.where(cls == 1.0, count_h, rows_h.astype(F32) - count_h)
            for b in range(8):
                place = (((i % 2) * 4 + b // 2) * 4 + i // 2) * 16
                rankh[b % 2, pl.ds(pl.multiple_of(place, 16), 16), :] = count_h[16 * b:16 * b + 16]
                clsb[b % 2, pl.ds(pl.multiple_of(place, 16), 16), :] = cls[16 * b:16 * b + 16]
            return carry

        lax.fori_loop(0, 8, chunk, 0)
        for h in range(2):
            row = jnp.transpose(rankh[h])[0:1]
            fold[h] = one_hot(lax.broadcasted_iota(jnp.int32, (CAPL, 512), 0).astype(F32) == row)

    def more_tables():
        for h in range(2):
            for t in range(3):
                w = min(128, CAPL - 128 * t)
                lane = lax.broadcasted_iota(jnp.int32, (512, w), 1).astype(F32) + 128.0 * t
                unfold[h, :, 128 * t:128 * t + w] = one_hot(rankh[h][:, :w] == lane)
        for t in range(MCAP // 128):
            lane = lax.broadcasted_iota(jnp.int32, (1024, 128), 1).astype(F32) + 128.0 * t
            foldb[:, 128 * t:128 * t + 128] = one_hot(rankb[...] == lane)
        crows = col[pl.ds(pl.multiple_of(32 * v, 32), 32), :]
        for par in range(2):
            for t in range(8):
                row = flip(vrow[:, 128 * t:128 * t + 128], col_irr + par)
                wmask[par, :, 128 * t:128 * t + 128] = one_hot(crows == row)
        sub = lax.broadcasted_iota(jnp.int32, (32, 128), 0)
        hit = sub == lax.broadcasted_iota(jnp.int32, (32, 128), 1) % 32
        crow[...] = jnp.sum(jnp.where(hit, crows, 0.0), axis=0, keepdims=True)

    def last_tables():
        row = jnp.transpose(rankb[...])[0:1]
        unfoldb[...] = one_hot(lax.broadcasted_iota(jnp.int32, (MCAP, 1024), 0).astype(F32) == row)

    def lane_class(src, k0, step):
        row = flip(crow[...], slab_irr + occ_ref[25 * src + k0])
        for q in range(1, 4):
            other = flip(crow[...], slab_irr + occ_ref[25 * src + k0 + q * step])
            row = jnp.where(lane128 // 32 == q, other, row)
        return row

    def prepare_w(i):
        w_copy(i).wait()

        def mask_k(k, carry):
            rows = pl.ds(pl.multiple_of(800 * i + 32 * k, 32), 32)
            wv[rows, :] = wv[rows, :] * wmask[occ_ref[25 * i + k]]
            return carry

        lax.fori_loop(0, 25, mask_k, 0, unroll=5)
        rows = pl.ds(pl.multiple_of(800 * i, 32), 800)
        value = jnp.dot(wv[rows, :], foldb[...], preferred_element_type=F32).astype(BF)
        for g in range(3):
            wf[g, i] = value[256 * g:256 * g + 256]
        for q in range(4):
            wrep[i, q] = value[768:800]

    rank_tables()
    more_tables()

    def relay(n):
        h, g = n // 3, n % 3
        for o in (1, 2, 3):
            y_copy(n, o).wait_recv()
        y_own(n).wait()
        b1 = (lane128 // 64) % 2 == 1
        b0 = (lane128 // 32) % 2 == 1
        for kg in range(2):
            rowsq = []
            for q in range(4):
                k = 8 * g + 4 * kg + q
                par = occ_ref[25 * x + k]
                rowsq.append((mbuf[h, k] * amask[h, par]).astype(F32))
            for t in range(2):
                res = block_transpose([r[:, 128 * t:128 * t + 128] for r in rowsq], b1, b0)
                for d in range(4):
                    sbuf[n, 4 * t + d, :, 128 * kg:128 * kg + 128] = res[d].astype(BF)
        for o in (4, 5, 2, 3, 6, 7, 1):
            z_copy(n, o).start()
        z_own(n).start()

        @pl.when(g == GL)
        def _():
            for o in (1, 2, 3):
                y_copyl(h, o).wait_recv()
            y_ownl(h).wait()
            par = occ_ref[25 * x + 24]
            whole = (mbuf[h, 24] * amask[h, par]).astype(F32)
            for t in range(2):
                res = block_transpose(
                    [whole[16 * q:16 * q + 16, 128 * t:128 * t + 128] for q in range(4)], b1, b0)
                for d in range(4):
                    sleft[h, 4 * t + d] = res[d].astype(BF)
            for o in (4, 5, 2, 3, 6, 7, 1):
                z_copyl(h, o).start()
            z_ownl(h).start()

    def fold_step(n):
        h, g = n // 3, n % 3
        for o in range(1, 8):
            z_copy(n, o).wait_recv()
        z_own(n).wait()
        xbuf[n, 0] = jnp.dot(fold[h, :CAP], abuf[n], preferred_element_type=F32).astype(BF)
        for side in range(2):
            x_copy(n, side).start()

        @pl.when(g == GL)
        def _():
            for o in range(1, 8):
                z_copyl(h, o).wait_recv()
            z_ownl(h).wait()
            got = aleft[h].astype(F32)
            parts = []
            for s in range(8):
                for q in range(4):
                    parts.append(jnp.where(lane128 // 32 == q, got[16 * s:16 * s + 16], 0.0))
            spread = jnp.concatenate(parts, axis=0).astype(BF)
            both = jnp.dot(fold[h], spread, preferred_element_type=F32)
            both = both + pltpu.roll(both, 64, 1)
            both = both + pltpu.roll(both, 32, 1)
            packed = both[0:80]
            for q in range(1, 4):
                packed = jnp.where(lane128 // 32 == q, both[80 * q:80 * q + 80], packed)
            xleft[h, 0] = packed.astype(BF)
            for side in range(2):
                x_copyl(h, side).start()

    def spread(n, slot):
        h, g = n // 3, n % 3
        src = (x + (0, 3, 1, 2)[slot]) % 4
        part = jnp.dot(unfold[h, :, :CAP], xbuf[n, slot], preferred_element_type=F32)
        cls = clsb[h]
        for t in range(2):
            piece = jnp.where(
                cls == lane_class(src, 8 * g + 4 * t, 1), part[:, 128 * t:128 * t + 128], 0.0).astype(BF)
            for i in range(8):
                wide[n % 2, i // 2, i % 2, :, pl.ds(pl.multiple_of(256 * src + 128 * t, 128), 128)] = (
                    piece[64 * i:64 * i + 64])

    def spread_left(h, slot):
        src = (x + (0, 3, 1, 2)[slot]) % 4
        got = xleft[h, slot].astype(F32)
        stacked = jnp.concatenate(
            [jnp.where(lane128 // 32 == q, got, 0.0) for q in range(4)], axis=0).astype(BF)
        part = jnp.dot(unfold[h], stacked, preferred_element_type=F32)
        part = jnp.where(clsb[h] == lane_class(src, 24, 0), part, 0.0).astype(BF)
        for i in range(8):
            widel[h, i // 2, i % 2, :, pl.ds(pl.multiple_of(128 * src, 128), 128)] = part[64 * i:64 * i + 64]

    def near_step(n):
        h, g = n // 3, n % 3
        for side in range(2):
            x_copy(n, side).wait_recv()
            f_copy(n, side).start()

        @pl.when(g == GL)
        def _():
            for side in range(2):
                x_copyl(h, side).wait_recv()

            @pl.when(h == 0)
            def _():
                f_copyl(h, 0).start()

            @pl.when(h == 1)
            def _():
                f_copyl(h, 1).start()

        for slot in range(3):
            spread(n, slot)

        @pl.when(g == GL)
        def _():
            for slot in range(3):
                spread_left(h, slot)

    def product(n, cc):
        h, g = n // 3, n % 3
        left_side = wide[n % 2, :, cc].reshape(256, 1024)
        value = jnp.dot(left_side, wf[g].reshape(1024, MCAP), preferred_element_type=F32).reshape(4, 64, MCAP)

        @pl.when(g == 0)
        def _():
            zacc[h, :, cc] = value

        @pl.when(g > 0)
        def _():
            zacc[h, :, cc] += value

    def far_step(n):
        h, g = n // 3, n % 3
        for side in range(2):
            f_copy(n, side).wait_recv()
        spread(n, 3)
        product(n, 1 - core)

        @pl.when(g == 2)
        def _():
            c_copy(h).start()

        product(n, core)

        @pl.when(g == GL)
        def _():
            f_copyl(h, 0).wait_recv()
            spread_left(h, 3)
            table = wrep[...].reshape(512, MCAP)
            for cc in range(2):
                zacc[h, :, cc] += jnp.dot(
                    widel[h, :, cc].reshape(256, 512), table, preferred_element_type=F32).reshape(4, 64, MCAP)

    def sum_core(h):
        c_copy(h).wait_recv()
        for zz in range(4):
            both = zacc[h, zz, core] + crecv[h, zz]
            for yy in range(4):
                for rh in range(2):
                    r0 = yy * 16 + rh * 8
                    tsum[h, rh, zz, yy] = both[r0:r0 + 8]
        for axis in range(2):
            for o in (2, 1, 3):
                r1_copy(h, axis, o).start()

    def sum_first(h):
        for axis in range(2):
            for o in (1, 2, 3):
                r1_copy(h, axis, o).wait_recv()
        for i in range(4):
            t2[h, 0, i] = tsum[h, 0, i, y] + r1buf[h, 0, 0, i] + r1buf[h, 0, 1, i] + r1buf[h, 0, 2, i]
            t2[h, 1, i] = tsum[h, 1, z, i] + r1buf[h, 1, 0, i] + r1buf[h, 1, 1, i] + r1buf[h, 1, 2, i]
        for axis in range(2):
            for o in (2, 1, 3):
                r2_copy(h, axis, o).start()

    def sum_second(h):
        for axis in range(2):
            for o in (1, 2, 3):
                r2_copy(h, axis, o).wait_recv()
        fin[h, 0] = t2[h, 0, z] + r2buf[h, 0, 0] + r2buf[h, 0, 1] + r2buf[h, 0, 2]
        fin[h, 1] = t2[h, 1, y] + r2buf[h, 1, 0] + r2buf[h, 1, 1] + r2buf[h, 1, 2]

    def step(n, carry):
        @pl.when(n < NSTEP)
        def _():
            relay(n)

        @pl.when(n == 0)
        def _():
            prepare_w(0)
            prepare_w(1)

        @pl.when(jnp.logical_and(n >= 1, n < NSTEP + 1))
        def _():
            fold_step(n - 1)

        @pl.when(n == 1)
        def _():
            prepare_w(2)

        @pl.when(n == 3)
        def _():
            last_tables()

        @pl.when(jnp.logical_and(n >= 2, n < NSTEP + 2))
        def _():
            near_step(n - 2)

        @pl.when(n == 2)
        def _():
            prepare_w(3)

        @pl.when(jnp.logical_or(n == 6, n == 9))
        def _():
            sum_core(n // 3 - 2)

        @pl.when(jnp.logical_and(n >= 3, n < NSTEP + 3))
        def _():
            far_step(n - 3)

        @pl.when(jnp.logical_or(n == 7, n == 10))
        def _():
            sum_first(n // 3 - 2)

        return carry

    lax.fori_loop(0, 11, step, 0)
    sum_second(0)
    sum_second(1)

    total = jnp.concatenate([fin[0, 0], fin[0, 1], fin[1, 0], fin[1, 1]], axis=0)
    hi = total.astype(BF)
    rest = total - hi.astype(F32)
    mid = rest.astype(BF)
    low = (rest - mid.astype(F32)).astype(BF)
    tile = evirt_ref[:, pl.ds(pl.multiple_of(128 * (v // 4), 128), 128)]
    e_rows = jnp.transpose(jnp.broadcast_to(tile, (128, 128)))
    ecol[...] = e_rows
    e_here = ecol[pl.ds(pl.multiple_of(32 * (v % 4), 32), 32), :]
    e_slab = eocc_ref[slab]
    e_col = eocc_ref[colo]
    cls = col[pl.ds(pl.multiple_of(32 * v, 32), 32), :]
    for t in range(8):
        lanes = slice(128 * t, 128 * t + 128)
        table = unfoldb[:, lanes]
        cycle_sum = (
            jnp.dot(hi, table, preferred_element_type=F32)
            + jnp.dot(mid, table, preferred_element_type=F32)
        ) + jnp.dot(low, table, preferred_element_type=F32)
        divisor = e_here + evirt_ref[:, lanes] - e_slab - e_col
        value = (drive_ref[:, lanes].astype(F32) + cycle_sum) / divisor
        out[0, :, 0, lanes] = jnp.where(cls == flip(vrow[:, lanes], slab_irr + col_irr), value, 0.0)

    def finish(n, carry):
        for o in (1, 2, 3):
            y_copy(n, o).wait_send()
        for o in range(1, 8):
            z_copy(n, o).wait_send()
        for side in range(2):
            x_copy(n, side).wait_send()
            f_copy(n, side).wait_send()
        return carry

    lax.fori_loop(0, NSTEP, finish, 0)

    def finish_half(h, carry):
        for o in (1, 2, 3):
            y_copyl(h, o).wait_send()
        for o in range(1, 8):
            z_copyl(h, o).wait_send()
        for side in range(2):
            x_copyl(h, side).wait_send()
        f_copyl(h, 0).wait_send()
        c_copy(h).wait_send()
        for axis in range(2):
            for o in (1, 2, 3):
                r1_copy(h, axis, o).wait_send()
                r2_copy(h, axis, o).wait_send()
        return carry

    lax.fori_loop(0, 2, finish_half, 0)


def folded_update(amp, wraw, drive, occ_irrep, virt_irrep, slab_occ, col_occ, occ_energy, virt_energy):
    dma = pltpu.SemaphoreType.DMA
    vmem = pl.BlockSpec(memory_space=pltpu.VMEM)
    hbm = pl.BlockSpec(memory_space=pl.ANY)
    smem = pltpu.SMEM
    scratch = [
        smem((100,), jnp.int32), smem((1,), jnp.int32), smem((4,), jnp.int32), smem((100,), F32),
        pltpu.VMEM((1, 1024), jnp.int32), pltpu.VMEM((1, 1024), F32), pltpu.VMEM((32, 1024), BF),
        pltpu.VMEM((3200, 1024), BF),
        pltpu.VMEM((3, 4, 256, MCAP), BF),
        pltpu.VMEM((4, 4, 32, MCAP), BF),
        pltpu.VMEM((2, 4, 2, 64, 1024), BF),
        pltpu.VMEM((2, 4, 2, 64, 512), BF),
        pltpu.VMEM((2, 2, 64, 256), BF),
        pltpu.VMEM((2, 32, 1024), BF),
        pltpu.VMEM((1, 1024), F32),
        pltpu.VMEM((1024, 128), F32),
        pltpu.VMEM((1, 128), F32),
        pltpu.VMEM((1024, 128), F32),
        pltpu.VMEM((2, 512, 128), F32),
        pltpu.VMEM((2, CAPL, 512), BF),
        pltpu.VMEM((2, 512, CAPL), BF),
        pltpu.VMEM((1024, MCAP), BF),
        pltpu.VMEM((MCAP, 1024), BF),
        pltpu.VMEM((2, 512, 128), F32),
        pltpu.VMEM((2, 25, 64, 256), BF),
        pltpu.VMEM((NSTEP, 8, 64, 256), BF),
        pltpu.VMEM((2, 8, 16, 128), BF),
        pltpu.VMEM((NSTEP, 512, 256), BF),
        pltpu.VMEM((2, 128, 128), BF),
        pltpu.VMEM((NSTEP, 4, CAP, 256), BF),
        pltpu.VMEM((2, 4, 80, 128), BF),
        pltpu.VMEM((2, 4, 2, 64, MCAP), F32),
        pltpu.VMEM((2, 4, 64, MCAP), F32),
        pltpu.VMEM((2, 2, 4, 4, 8, MCAP), F32),
        pltpu.VMEM((2, 2, 4, 8, MCAP), F32),
        pltpu.VMEM((2, 2, 3, 4, 8, MCAP), F32),
        pltpu.VMEM((2, 2, 3, 8, MCAP), F32),
        pltpu.VMEM((2, 2, 8, MCAP), F32),
        pltpu.VMEM((128, 128), F32),
        dma((7,)), dma((4,)),
        dma((NSTEP, 3)), dma((NSTEP, 3)), dma((NSTEP,)),
        dma((2, 3)), dma((2, 3)), dma((2,)),
        dma((NSTEP, 7)), dma((NSTEP, 7)), dma((NSTEP,)),
        dma((2, 7)), dma((2, 7)), dma((2,)),
        dma((NSTEP, 2)), dma((NSTEP, 2)), dma((NSTEP, 2)), dma((NSTEP, 2)),
        dma((2, 2)), dma((2, 2)), dma((2,)), dma((2,)),
        dma((2,)), dma((2,)),
        dma((2, 6)), dma((2, 6)), dma((2, 6)), dma((2, 6)),
    ]
    return pl.pallas_call(
        kernel,
        out_shape=(jax.ShapeDtypeStruct(OUT, F32), jax.ShapeDtypeStruct((1,), jnp.int32)),
        in_specs=[hbm] * 9,
        out_specs=(vmem, pl.BlockSpec(memory_space=smem)),
        scratch_shapes=scratch,
        compiler_params=pltpu.CompilerParams(
            collective_id=0, has_side_effects=True, vmem_limit_bytes=56 * 2**20
        ),
        name="cycle",
    )(occ_irrep, slab_occ, col_occ, occ_energy, virt_irrep.reshape(1, 1024), virt_energy.reshape(1, 1024),
      drive, amp, wraw)


def body(
    amplitudes,
    cycle_block,
    drive_term,
    occ_energy,
    virt_energy,
    occ_irrep,
    virt_irrep,
    slab_occ,
    col_occ,
):
    amp = amplitudes.reshape(25, 32, 1024)
    wraw = jnp.transpose(cycle_block, (1, 2, 0, 3)).reshape(3200, 1024)
    drive = jnp.transpose(drive_term, (0, 2, 1, 3)).reshape(32, 1024)
    amp, wraw, drive = lax.optimization_barrier((amp, wraw, drive))
    args = (amp, wraw, drive, occ_irrep, virt_irrep, slab_occ, col_occ, occ_energy, virt_energy)
    folded, fits = folded_update(*args)
    return lax.cond(fits[0] == 1, lambda value, *rest: value, lambda value, *rest: general_update(*rest), folded, *args)


def solution(mesh):
    in_specs = (
        P(None, "occ", "virt", None),
        P("virt", None, "occ", None),
        P(None, "virt", "occ", None),
        P(),
        P(),
        P(),
        P(),
        P(),
        P(),
    )
    out_specs = P(None, "virt", "occ", None)
    return jax.shard_map(body, mesh=mesh, in_specs=in_specs, out_specs=out_specs, check_vma=False)
```

```python
import jax
import jax.numpy as jnp
from jax import lax
from jax.experimental import pallas as pl
from jax.experimental.pallas import tpu as pltpu
from jax.sharding import PartitionSpec as P

MESH = pl.DeviceIdType.MESH
CAP = 304
CAPL = 320
MCAP = 640
NSTEP = 6
OUT = (1, 32, 1, 1024)
GL = 1
BF = jnp.bfloat16
F32 = jnp.float32


def pick_entries(values_table, indices):
    hits = indices[:, None] == jnp.arange(values_table.shape[0], dtype=jnp.int32)[None, :]
    return jnp.sum(
        jnp.where(hits, values_table[None, :], jnp.zeros((), values_table.dtype)), axis=1
    )


def spread_all(block, axis, count):
    return lax.all_to_all(jnp.broadcast_to(block[None], (count,) + block.shape), axis, 0, 0, tiled=True)


def general_update(amp, wraw, drive, occ_irrep, virt_irrep, slab_occ, col_occ, occ_energy, virt_energy):
    x = lax.axis_index("occ")
    v = lax.axis_index("virt")
    slab_irrep = pick_entries(occ_irrep, slab_occ)[0]
    col_here = lax.dynamic_slice_in_dim(col_occ, x, 1)
    col_irrep = pick_entries(occ_irrep, col_here)[0]
    irr_k = lax.dynamic_slice_in_dim(occ_irrep, x * 25, 25)
    irr_a = lax.dynamic_slice_in_dim(virt_irrep, v * 32, 32)
    parity = slab_irrep + irr_k[:, None, None] + irr_a[None, :, None] + virt_irrep[None, None, :]
    masked = jnp.where(parity % 2 == 0, amp, jnp.zeros((), amp.dtype))
    pair_block = spread_all(masked, "occ", 4).reshape(100, 32, 1024)
    relaid = lax.all_to_all(pair_block, "virt", split_axis=2, concat_axis=1, tiled=True)
    w = wraw.reshape(100, 32, 1024)
    partial_value = jnp.einsum("kac,kcb->ab", relaid, w, preferred_element_type=F32)
    parts = lax.all_to_all(partial_value.reshape(32, 32, 1024), "virt", 0, 0, tiled=True)
    cycle_sum = jnp.sum(parts, axis=0)
    e_slab = pick_entries(occ_energy, slab_occ)[0]
    e_col = pick_entries(occ_energy, col_here)[0]
    e_rows = lax.dynamic_slice_in_dim(virt_energy, v * 32, 32)
    divisor = e_rows[:, None] + virt_energy[None, :] - e_slab - e_col
    out_parity = slab_irrep + irr_a[:, None] + col_irrep + virt_irrep[None, :]
    value = (drive.astype(F32) + cycle_sum) / divisor
    return jnp.where(out_parity % 2 == 0, value, jnp.zeros((), F32)).reshape(OUT)


def block_transpose(tiles, b1, b0):
    t = list(tiles)
    for q in (0, 1):
        a, b = t[q], t[q + 2]
        t[q] = jnp.where(b1, pltpu.roll(b, 64, 1), a)
        t[q + 2] = jnp.where(b1, b, pltpu.roll(a, 64, 1))
    for q in (0, 2):
        a, b = t[q], t[q + 1]
        t[q] = jnp.where(b0, pltpu.roll(b, 32, 1), a)
        t[q + 1] = jnp.where(b0, b, pltpu.roll(a, 96, 1))
    return t


def kernel(
    occ_in, slab_in, colo_in, eocc_in, virt_in, evirt_in, drive_in, amp, wraw,
    out, fits_ref,
    occ_ref, slab_ref, colo_ref, eocc_ref, virt_ref, evirt_ref, drive_ref,
    wv, wf, wrep, wide, widel, amask, wmask, vrow, col, crow, rankb, rankh, fold, unfold, foldb, unfoldb, clsb, mbuf, sbuf, sleft, abuf, aleft,
    xbuf, xleft, zacc, crecv, tsum, t2, r1buf, r2buf, fin, ecol,
    insem, wsem, ysend, yrecv, yloc, ysendl, yrecvl, ylocl,
    zsend, zrecv, zloc, zsendl, zrecvl, zlocl,
    xsend, xrecv, fsend, frecv, xsendl, xrecvl, fsendl, frecvl,
    csend, crecvs, r1send, r1recv, r2send, r2recv,
):
    x = lax.axis_index("occ")
    v = lax.axis_index("virt")
    y = v // 8
    z = (v // 2) % 4
    core = v % 2
    me8 = z * 2 + core

    def virt_at(yy, zz, cc):
        return (yy * 4 + zz) * 2 + cc

    right = (x + 1) % 4
    left = (x + 3) % 4

    def y_peer(o):
        return (x, virt_at((y + o) % 4, z, core))

    def z_peer(o):
        oz, oc = o // 2, o % 2
        return (x, virt_at(y, (z + oz) % 4, (core + oc) % 2))

    def z_slot(o):
        return ((z + o // 2) % 4) * 2 + (core + o % 2) % 2

    def remote(src, dst, ssem, rsem, dev):
        return pltpu.make_async_remote_copy(
            src_ref=src, dst_ref=dst, send_sem=ssem, recv_sem=rsem,
            device_id=dev, device_id_type=MESH,
        )

    def y_src(h, k0, nk, yd):
        return amp.at[pl.ds(k0, nk), pl.ds(16 * h, 16), pl.ds(pl.multiple_of(256 * yd, 256), 256)]

    def y_dst(h, k0, nk):
        return mbuf.at[h, pl.ds(k0, nk), pl.ds(pl.multiple_of(16 * y, 16), 16), :]

    def y_copy(n, o):
        h, g = n // 3, n % 3
        return remote(y_src(h, 8 * g, 8, (y + o) % 4), y_dst(h, 8 * g, 8),
                      ysend.at[n, o - 1], yrecv.at[n, o - 1], y_peer(o))

    def y_copyl(h, o):
        return remote(y_src(h, 24, 1, (y + o) % 4), y_dst(h, 24, 1),
                      ysendl.at[h, o - 1], yrecvl.at[h, o - 1], y_peer(o))

    def y_own(n):
        h, g = n // 3, n % 3
        return pltpu.make_async_copy(y_src(h, 8 * g, 8, y), y_dst(h, 8 * g, 8), yloc.at[n])

    def y_ownl(h):
        return pltpu.make_async_copy(y_src(h, 24, 1, y), y_dst(h, 24, 1), ylocl.at[h])

    def z_dst(n):
        return abuf.at[n, pl.ds(pl.multiple_of(64 * me8, 64), 64), :]

    def z_dstl(h):
        return aleft.at[h, pl.ds(pl.multiple_of(16 * me8, 16), 16), :]

    def z_copy(n, o):
        return remote(sbuf.at[n, z_slot(o)], z_dst(n), zsend.at[n, o - 1], zrecv.at[n, o - 1], z_peer(o))

    def z_copyl(h, o):
        return remote(sleft.at[h, z_slot(o)], z_dstl(h), zsendl.at[h, o - 1], zrecvl.at[h, o - 1], z_peer(o))

    def z_own(n):
        return pltpu.make_async_copy(sbuf.at[n, me8], z_dst(n), zloc.at[n])

    def z_ownl(h):
        return pltpu.make_async_copy(sleft.at[h, me8], z_dstl(h), zlocl.at[h])

    def x_copy(n, side):
        return remote(xbuf.at[n, 0], xbuf.at[n, 1 + side], xsend.at[n, side], xrecv.at[n, side],
                      ((right, left)[side], v))

    def f_copy(n, side):
        lanes = pl.ds(128 * side, 128)
        return remote(xbuf.at[n, 1 + side, :, lanes], xbuf.at[n, 3, :, lanes],
                      fsend.at[n, side], frecv.at[n, side], ((right, left)[side], v))

    def x_copyl(h, side):
        return remote(xleft.at[h, 0], xleft.at[h, 1 + side], xsendl.at[h, side], xrecvl.at[h, side],
                      ((right, left)[side], v))

    def f_copyl(h, side):
        return remote(xleft.at[h, 1 + side], xleft.at[h, 3], fsendl.at[h], frecvl.at[h],
                      ((right, left)[side], v))

    def c_copy(h):
        return remote(zacc.at[h, :, 1 - core], crecv.at[h], csend.at[h], crecvs.at[h],
                      (x, virt_at(y, z, 1 - core)))

    def r1_copy(h, axis, o):
        if axis == 0:
            yd = (y + o) % 4
            return remote(tsum.at[h, 0, :, yd], r1buf.at[h, 0, o - 1], r1send.at[h, o - 1],
                          r1recv.at[h, o - 1], (x, virt_at(yd, z, core)))
        zd = (z + o) % 4
        return remote(tsum.at[h, 1, zd], r1buf.at[h, 1, o - 1], r1send.at[h, 2 + o],
                      r1recv.at[h, 2 + o], (x, virt_at(y, zd, core)))

    def r2_copy(h, axis, o):
        if axis == 0:
            zd = (z + o) % 4
            return remote(t2.at[h, 0, zd], r2buf.at[h, 0, o - 1], r2send.at[h, o - 1],
                          r2recv.at[h, o - 1], (x, virt_at(y, zd, core)))
        yd = (y + o) % 4
        return remote(t2.at[h, 1, yd], r2buf.at[h, 1, o - 1], r2send.at[h, 2 + o],
                      r2recv.at[h, 2 + o], (x, virt_at(yd, z, core)))

    loads = [
        pltpu.make_async_copy(src, dst, insem.at[i])
        for i, (src, dst) in enumerate((
            (occ_in, occ_ref), (slab_in, slab_ref), (colo_in, colo_ref), (eocc_in, eocc_ref),
            (virt_in, virt_ref), (evirt_in, evirt_ref), (drive_in, drive_ref)))
    ]
    for load in loads:
        load.start()

    barrier = pltpu.get_barrier_semaphore()
    peers = [y_peer(o) for o in (1, 2, 3)] + [z_peer(o) for o in range(1, 8)] + [(right, v), (left, v)]
    for dev in peers:
        pl.semaphore_signal(barrier, inc=1, device_id=dev, device_id_type=MESH)
    pl.semaphore_wait(barrier, len(peers))

    def w_copy(i):
        rows = pl.ds(800 * i, 800)
        return pltpu.make_async_copy(wraw.at[rows], wv.at[rows], wsem.at[i])

    for n in range(NSTEP):
        for o in (2, 1, 3):
            y_copy(n, o).start()
        y_own(n).start()
        if n % 3 == GL:
            for o in (2, 1, 3):
                y_copyl(n // 3, o).start()
            y_ownl(n // 3).start()
        if n == 1:
            for i in range(4):
                w_copy(i).start()

    lane128 = lax.broadcasted_iota(jnp.int32, (1, 128), 1)

    for load in loads:
        load.wait()
    slab = slab_ref[0]
    slab_irr = occ_ref[slab]
    colo = colo_ref[x]
    col_irr = occ_ref[colo]

    def flip(row, par):
        return jnp.where(par % 2 == 1, 1.0 - row, row)

    def one_hot(cond):
        return cond.astype(F32).astype(BF)

    vrow[...] = virt_ref[...].astype(F32)
    col[...] = jnp.transpose(jnp.broadcast_to(vrow[...], (128, 1024)))
    second = (lax.broadcasted_iota(jnp.int32, (1, 1024), 1) & 16) != 0
    ones_b = jnp.sum(jnp.where(second, vrow[...], 0.0))
    ones_a = jnp.sum(vrow[...]) - ones_b
    total = ones_a + ones_b
    fits = (
        (ones_a <= CAP) & (ones_a >= 512 - CAP) & (ones_b <= CAP) & (ones_b >= 512 - CAP)
        & (total <= MCAP) & (total >= 1024 - MCAP)
    )
    fits_ref[0] = fits.astype(jnp.int32)
    for h in range(2):
        rows = jnp.concatenate(
            [col[pl.ds(pl.multiple_of(256 * yy + 32 * (me8) + 16 * h, 16), 16), :] for yy in range(4)], axis=0)
        for t in range(2):
            c_mid = vrow[:, pl.ds(pl.multiple_of(256 * y + 128 * t, 128), 128)]
            for par in range(2):
                amask[h, par, :, 128 * t:128 * t + 128] = one_hot(rows == flip(c_mid, slab_irr + par))

    def rank_tables():
        def chunk(i, carry):
            rows = lax.broadcasted_iota(jnp.int32, (128, 1024), 0) + 128 * i
            cols = lax.broadcasted_iota(jnp.int32, (128, 1024), 1)
            before = cols < rows
            ones = col[...].astype(BF)
            count = jnp.dot(one_hot(before), ones, preferred_element_type=F32)
            same = ((rows ^ cols) & 16) == 0
            count_h = jnp.dot(one_hot(before & same), ones, preferred_element_type=F32)
            here = pl.ds(pl.multiple_of(128 * i, 128), 128)
            cls = col[here, :]
            rows = lax.broadcasted_iota(jnp.int32, (128, 128), 0) + 128 * i
            rankb[here, :] = jnp.where(cls == 1.0, count, rows.astype(F32) - count)
            rows_h = (rows >> 5) * 16 + (rows & 15)
            count_h = jnp.where(cls == 1.0, count_h, rows_h.astype(F32) - count_h)
            for b in range(8):
                place = (((i % 2) * 4 + b // 2) * 4 + i // 2) * 16
                rankh[b % 2, pl.ds(pl.multiple_of(place, 16), 16), :] = count_h[16 * b:16 * b + 16]
                clsb[b % 2, pl.ds(pl.multiple_of(place, 16), 16), :] = cls[16 * b:16 * b + 16]
            return carry

        lax.fori_loop(0, 8, chunk, 0)
        for h in range(2):
            row = jnp.transpose(rankh[h])[0:1]
            fold[h] = one_hot(lax.broadcasted_iota(jnp.int32, (CAPL, 512), 0).astype(F32) == row)

    def more_tables():
        for h in range(2):
            for t in range(3):
                w = min(128, CAPL - 128 * t)
                lane = lax.broadcasted_iota(jnp.int32, (512, w), 1).astype(F32) + 128.0 * t
                unfold[h, :, 128 * t:128 * t + w] = one_hot(rankh[h][:, :w] == lane)
        for t in range(MCAP // 128):
            lane = lax.broadcasted_iota(jnp.int32, (1024, 128), 1).astype(F32) + 128.0 * t
            foldb[:, 128 * t:128 * t + 128] = one_hot(rankb[...] == lane)
        crows = col[pl.ds(pl.multiple_of(32 * v, 32), 32), :]
        for par in range(2):
            for t in range(8):
                row = flip(vrow[:, 128 * t:128 * t + 128], col_irr + par)
                wmask[par, :, 128 * t:128 * t + 128] = one_hot(crows == row)
        sub = lax.broadcasted_iota(jnp.int32, (32, 128), 0)
        hit = sub == lax.broadcasted_iota(jnp.int32, (32, 128), 1) % 32
        crow[...] = jnp.sum(jnp.where(hit, crows, 0.0), axis=0, keepdims=True)

    def last_tables():
        row = jnp.transpose(rankb[...])[0:1]
        unfoldb[...] = one_hot(lax.broadcasted_iota(jnp.int32, (MCAP, 1024), 0).astype(F32) == row)

    def lane_class(src, k0, step):
        row = flip(crow[...], slab_irr + occ_ref[25 * src + k0])
        for q in range(1, 4):
            other = flip(crow[...], slab_irr + occ_ref[25 * src + k0 + q * step])
            row = jnp.where(lane128 // 32 == q, other, row)
        return row

    def prepare_w(i):
        w_copy(i).wait()

        def mask_k(k, carry):
            rows = pl.ds(pl.multiple_of(800 * i + 32 * k, 32), 32)
            wv[rows, :] = wv[rows, :] * wmask[occ_ref[25 * i + k]]
            return carry

        lax.fori_loop(0, 25, mask_k, 0, unroll=5)
        rows = pl.ds(pl.multiple_of(800 * i, 32), 800)
        value = jnp.dot(wv[rows, :], foldb[...], preferred_element_type=F32).astype(BF)
        for g in range(3):
            wf[g, i] = value[256 * g:256 * g + 256]
        for q in range(4):
            wrep[i, q] = value[768:800]

    rank_tables()
    more_tables()

    def relay(n):
        h, g = n // 3, n % 3
        for o in (1, 2, 3):
            y_copy(n, o).wait_recv()
        y_own(n).wait()
        b1 = (lane128 // 64) % 2 == 1
        b0 = (lane128 // 32) % 2 == 1
        for kg in range(2):
            rowsq = []
            for q in range(4):
                k = 8 * g + 4 * kg + q
                par = occ_ref[25 * x + k]
                rowsq.append((mbuf[h, k] * amask[h, par]).astype(F32))
            for t in range(2):
                res = block_transpose([r[:, 128 * t:128 * t + 128] for r in rowsq], b1, b0)
                for d in range(4):
                    sbuf[n, 4 * t + d, :, 128 * kg:128 * kg + 128] = res[d].astype(BF)
        for o in (4, 5, 2, 3, 6, 7, 1):
            z_copy(n, o).start()
        z_own(n).start()

        @pl.when(g == GL)
        def _():
            for o in (1, 2, 3):
                y_copyl(h, o).wait_recv()
            y_ownl(h).wait()
            par = occ_ref[25 * x + 24]
            whole = (mbuf[h, 24] * amask[h, par]).astype(F32)
            for t in range(2):
                res = block_transpose(
                    [whole[16 * q:16 * q + 16, 128 * t:128 * t + 128] for q in range(4)], b1, b0)
                for d in range(4):
                    sleft[h, 4 * t + d] = res[d].astype(BF)
            for o in (4, 5, 2, 3, 6, 7, 1):
                z_copyl(h, o).start()
            z_ownl(h).start()

    def fold_step(n):
        h, g = n // 3, n % 3
        for o in range(1, 8):
            z_copy(n, o).wait_recv()
        z_own(n).wait()
        xbuf[n, 0] = jnp.dot(fold[h, :CAP], abuf[n], preferred_element_type=F32).astype(BF)
        for side in range(2):
            x_copy(n, side).start()

        @pl.when(g == GL)
        def _():
            for o in range(1, 8):
                z_copyl(h, o).wait_recv()
            z_ownl(h).wait()
            got = aleft[h].astype(F32)
            parts = []
            for s in range(8):
                for q in range(4):
                    parts.append(jnp.where(lane128 // 32 == q, got[16 * s:16 * s + 16], 0.0))
            spread = jnp.concatenate(parts, axis=0).astype(BF)
            both = jnp.dot(fold[h], spread, preferred_element_type=F32)
            both = both + pltpu.roll(both, 64, 1)
            both = both + pltpu.roll(both, 32, 1)
            packed = both[0:80]
            for q in range(1, 4):
                packed = jnp.where(lane128 // 32 == q, both[80 * q:80 * q + 80], packed)
            xleft[h, 0] = packed.astype(BF)
            for side in range(2):
                x_copyl(h, side).start()

    def spread(n, slot):
        h, g = n // 3, n % 3
        src = (x + (0, 3, 1, 2)[slot]) % 4
        part = jnp.dot(unfold[h, :, :CAP], xbuf[n, slot], preferred_element_type=F32)
        cls = clsb[h]
        for t in range(2):
            piece = jnp.where(
                cls == lane_class(src, 8 * g + 4 * t, 1), part[:, 128 * t:128 * t + 128], 0.0).astype(BF)
            for i in range(8):
                wide[n % 2, i // 2, i % 2, :, pl.ds(pl.multiple_of(256 * src + 128 * t, 128), 128)] = (
                    piece[64 * i:64 * i + 64])

    def spread_left(h, slot):
        src = (x + (0, 3, 1, 2)[slot]) % 4
        got = xleft[h, slot].astype(F32)
        stacked = jnp.concatenate(
            [jnp.where(lane128 // 32 == q, got, 0.0) for q in range(4)], axis=0).astype(BF)
        part = jnp.dot(unfold[h], stacked, preferred_element_type=F32)
        part = jnp.where(clsb[h] == lane_class(src, 24, 0), part, 0.0).astype(BF)
        for i in range(8):
            widel[h, i // 2, i % 2, :, pl.ds(pl.multiple_of(128 * src, 128), 128)] = part[64 * i:64 * i + 64]

    def near_step(n):
        h, g = n // 3, n % 3
        for side in range(2):
            x_copy(n, side).wait_recv()
            f_copy(n, side).start()

        @pl.when(g == GL)
        def _():
            for side in range(2):
                x_copyl(h, side).wait_recv()

            @pl.when(h == 0)
            def _():
                f_copyl(h, 0).start()

            @pl.when(h == 1)
            def _():
                f_copyl(h, 1).start()

        for slot in range(3):
            spread(n, slot)

        @pl.when(g == GL)
        def _():
            for slot in range(3):
                spread_left(h, slot)

    def product(n, cc):
        h, g = n // 3, n % 3
        left_side = wide[n % 2, :, cc].reshape(256, 1024)
        value = jnp.dot(left_side, wf[g].reshape(1024, MCAP), preferred_element_type=F32).reshape(4, 64, MCAP)

        @pl.when(g == 0)
        def _():
            zacc[h, :, cc] = value

        @pl.when(g > 0)
        def _():
            zacc[h, :, cc] += value

    def far_step(n):
        h, g = n // 3, n % 3
        for side in range(2):
            f_copy(n, side).wait_recv()
        spread(n, 3)
        product(n, 1 - core)

        @pl.when(g == 2)
        def _():
            c_copy(h).start()

        product(n, core)

        @pl.when(g == GL)
        def _():
            f_copyl(h, 0).wait_recv()
            spread_left(h, 3)
            table = wrep[...].reshape(512, MCAP)
            for cc in range(2):
                zacc[h, :, cc] += jnp.dot(
                    widel[h, :, cc].reshape(256, 512), table, preferred_element_type=F32).reshape(4, 64, MCAP)

    def sum_core(h):
        c_copy(h).wait_recv()
        for zz in range(4):
            both = zacc[h, zz, core] + crecv[h, zz]
            for yy in range(4):
                for rh in range(2):
                    r0 = yy * 16 + rh * 8
                    tsum[h, rh, zz, yy] = both[r0:r0 + 8]
        for axis in range(2):
            for o in (2, 1, 3):
                r1_copy(h, axis, o).start()

    def sum_first(h):
        for axis in range(2):
            for o in (1, 2, 3):
                r1_copy(h, axis, o).wait_recv()
        for i in range(4):
            t2[h, 0, i] = tsum[h, 0, i, y] + r1buf[h, 0, 0, i] + r1buf[h, 0, 1, i] + r1buf[h, 0, 2, i]
            t2[h, 1, i] = tsum[h, 1, z, i] + r1buf[h, 1, 0, i] + r1buf[h, 1, 1, i] + r1buf[h, 1, 2, i]
        for axis in range(2):
            for o in (2, 1, 3):
                r2_copy(h, axis, o).start()

    def sum_second(h):
        for axis in range(2):
            for o in (1, 2, 3):
                r2_copy(h, axis, o).wait_recv()
        fin[h, 0] = t2[h, 0, z] + r2buf[h, 0, 0] + r2buf[h, 0, 1] + r2buf[h, 0, 2]
        fin[h, 1] = t2[h, 1, y] + r2buf[h, 1, 0] + r2buf[h, 1, 1] + r2buf[h, 1, 2]

    prepare_w(0)

    def step(n, carry):
        @pl.when(n < NSTEP)
        def _():
            relay(n)

        @pl.when(n == 0)
        def _():
            prepare_w(1)

        @pl.when(jnp.logical_and(n >= 1, n < NSTEP + 1))
        def _():
            fold_step(n - 1)

        @pl.when(n == 1)
        def _():
            prepare_w(2)

        @pl.when(n == 3)
        def _():
            last_tables()

        @pl.when(jnp.logical_and(n >= 2, n < NSTEP + 2))
        def _():
            near_step(n - 2)

        @pl.when(n == 2)
        def _():
            prepare_w(3)

        @pl.when(jnp.logical_or(n == 6, n == 9))
        def _():
            sum_core(n // 3 - 2)

        @pl.when(jnp.logical_and(n >= 3, n < NSTEP + 3))
        def _():
            far_step(n - 3)

        @pl.when(n == 9)
        def _():
            sum_second(0)

        @pl.when(jnp.logical_or(n == 7, n == 10))
        def _():
            sum_first(n // 3 - 2)

        return carry

    lax.fori_loop(0, 11, step, 0)
    sum_second(1)

    total = jnp.concatenate([fin[0, 0], fin[0, 1], fin[1, 0], fin[1, 1]], axis=0)
    hi = total.astype(BF)
    rest = total - hi.astype(F32)
    mid = rest.astype(BF)
    low = (rest - mid.astype(F32)).astype(BF)
    tile = evirt_ref[:, pl.ds(pl.multiple_of(128 * (v // 4), 128), 128)]
    e_rows = jnp.transpose(jnp.broadcast_to(tile, (128, 128)))
    ecol[...] = e_rows
    e_here = ecol[pl.ds(pl.multiple_of(32 * (v % 4), 32), 32), :]
    e_slab = eocc_ref[slab]
    e_col = eocc_ref[colo]
    cls = col[pl.ds(pl.multiple_of(32 * v, 32), 32), :]
    parts = jnp.concatenate([hi.astype(F32), mid.astype(F32), low.astype(F32)], axis=0).astype(BF)
    spread_out = jnp.dot(parts, unfoldb[...], preferred_element_type=F32)
    for t in range(8):
        lanes = slice(128 * t, 128 * t + 128)
        cycle_sum = (spread_out[0:32, lanes] + spread_out[32:64, lanes]) + spread_out[64:96, lanes]
        divisor = e_here + evirt_ref[:, lanes] - e_slab - e_col
        value = (drive_ref[:, lanes].astype(F32) + cycle_sum) / divisor
        out[0, :, 0, lanes] = jnp.where(cls == flip(vrow[:, lanes], slab_irr + col_irr), value, 0.0)

    def finish(n, carry):
        for o in (1, 2, 3):
            y_copy(n, o).wait_send()
        for o in range(1, 8):
            z_copy(n, o).wait_send()
        for side in range(2):
            x_copy(n, side).wait_send()
            f_copy(n, side).wait_send()
        return carry

    lax.fori_loop(0, NSTEP, finish, 0)

    def finish_half(h, carry):
        for o in (1, 2, 3):
            y_copyl(h, o).wait_send()
        for o in range(1, 8):
            z_copyl(h, o).wait_send()
        for side in range(2):
            x_copyl(h, side).wait_send()
        f_copyl(h, 0).wait_send()
        c_copy(h).wait_send()
        for axis in range(2):
            for o in (1, 2, 3):
                r1_copy(h, axis, o).wait_send()
                r2_copy(h, axis, o).wait_send()
        return carry

    lax.fori_loop(0, 2, finish_half, 0)


def folded_update(amp, wraw, drive, occ_irrep, virt_irrep, slab_occ, col_occ, occ_energy, virt_energy):
    dma = pltpu.SemaphoreType.DMA
    vmem = pl.BlockSpec(memory_space=pltpu.VMEM)
    hbm = pl.BlockSpec(memory_space=pl.ANY)
    smem = pltpu.SMEM
    scratch = [
        smem((100,), jnp.int32), smem((1,), jnp.int32), smem((4,), jnp.int32), smem((100,), F32),
        pltpu.VMEM((1, 1024), jnp.int32), pltpu.VMEM((1, 1024), F32), pltpu.VMEM((32, 1024), BF),
        pltpu.VMEM((3200, 1024), BF),
        pltpu.VMEM((3, 4, 256, MCAP), BF),
        pltpu.VMEM((4, 4, 32, MCAP), BF),
        pltpu.VMEM((2, 4, 2, 64, 1024), BF),
        pltpu.VMEM((2, 4, 2, 64, 512), BF),
        pltpu.VMEM((2, 2, 64, 256), BF),
        pltpu.VMEM((2, 32, 1024), BF),
        pltpu.VMEM((1, 1024), F32),
        pltpu.VMEM((1024, 128), F32),
        pltpu.VMEM((1, 128), F32),
        pltpu.VMEM((1024, 128), F32),
        pltpu.VMEM((2, 512, 128), F32),
        pltpu.VMEM((2, CAPL, 512), BF),
        pltpu.VMEM((2, 512, CAPL), BF),
        pltpu.VMEM((1024, MCAP), BF),
        pltpu.VMEM((MCAP, 1024), BF),
        pltpu.VMEM((2, 512, 128), F32),
        pltpu.VMEM((2, 25, 64, 256), BF),
        pltpu.VMEM((NSTEP, 8, 64, 256), BF),
        pltpu.VMEM((2, 8, 16, 128), BF),
        pltpu.VMEM((NSTEP, 512, 256), BF),
        pltpu.VMEM((2, 128, 128), BF),
        pltpu.VMEM((NSTEP, 4, CAP, 256), BF),
        pltpu.VMEM((2, 4, 80, 128), BF),
        pltpu.VMEM((2, 4, 2, 64, MCAP), F32),
        pltpu.VMEM((2, 4, 64, MCAP), F32),
        pltpu.VMEM((2, 2, 4, 4, 8, MCAP), F32),
        pltpu.VMEM((2, 2, 4, 8, MCAP), F32),
        pltpu.VMEM((2, 2, 3, 4, 8, MCAP), F32),
        pltpu.VMEM((2, 2, 3, 8, MCAP), F32),
        pltpu.VMEM((2, 2, 8, MCAP), F32),
        pltpu.VMEM((128, 128), F32),
        dma((7,)), dma((4,)),
        dma((NSTEP, 3)), dma((NSTEP, 3)), dma((NSTEP,)),
        dma((2, 3)), dma((2, 3)), dma((2,)),
        dma((NSTEP, 7)), dma((NSTEP, 7)), dma((NSTEP,)),
        dma((2, 7)), dma((2, 7)), dma((2,)),
        dma((NSTEP, 2)), dma((NSTEP, 2)), dma((NSTEP, 2)), dma((NSTEP, 2)),
        dma((2, 2)), dma((2, 2)), dma((2,)), dma((2,)),
        dma((2,)), dma((2,)),
        dma((2, 6)), dma((2, 6)), dma((2, 6)), dma((2, 6)),
    ]
    return pl.pallas_call(
        kernel,
        out_shape=(jax.ShapeDtypeStruct(OUT, F32), jax.ShapeDtypeStruct((1,), jnp.int32)),
        in_specs=[hbm] * 9,
        out_specs=(vmem, pl.BlockSpec(memory_space=smem)),
        scratch_shapes=scratch,
        compiler_params=pltpu.CompilerParams(
            collective_id=0, has_side_effects=True, vmem_limit_bytes=56 * 2**20
        ),
        name="cycle",
    )(occ_irrep, slab_occ, col_occ, occ_energy, virt_irrep.reshape(1, 1024), virt_energy.reshape(1, 1024),
      drive, amp, wraw)


def body(
    amplitudes,
    cycle_block,
    drive_term,
    occ_energy,
    virt_energy,
    occ_irrep,
    virt_irrep,
    slab_occ,
    col_occ,
):
    amp = amplitudes.reshape(25, 32, 1024)
    wraw = jnp.transpose(cycle_block, (1, 2, 0, 3)).reshape(3200, 1024)
    drive = jnp.transpose(drive_term, (0, 2, 1, 3)).reshape(32, 1024)
    amp, wraw, drive = lax.optimization_barrier((amp, wraw, drive))
    args = (amp, wraw, drive, occ_irrep, virt_irrep, slab_occ, col_occ, occ_energy, virt_energy)
    folded, fits = folded_update(*args)
    return lax.cond(fits[0] == 1, lambda value, *rest: value, lambda value, *rest: general_update(*rest), folded, *args)


def solution(mesh):
    in_specs = (
        P(None, "occ", "virt", None),
        P("virt", None, "occ", None),
        P(None, "virt", "occ", None),
        P(),
        P(),
        P(),
        P(),
        P(),
        P(),
    )
    out_specs = P(None, "virt", "occ", None)
    return jax.shard_map(body, mesh=mesh, in_specs=in_specs, out_specs=out_specs, check_vma=False)
```
